32 devices in a mesh: ctx: 8 (over y, x, core), tp: 4 (over z).
Axes of the slice: x: 2, y: 2, z: 4, core: 2. Of those that a mesh axis runs over, the one named last changes fastest.
Arguments:
- query: bfloat16 [8192, 4096], P('ctx', 'tp'), may hold values from -6 to 6
- keys: bfloat16 [8192, 4096], P('ctx', 'tp'), may hold values from -6 to 6
- values: bfloat16 [8192, 4096], P('ctx', 'tp'), may hold values from -6 to 6
- residues: float32 [256, 16], replicated, may hold values from -1.5 to 1.5
- rates: float32 [256, 16], replicated, as said below
- w_out: bfloat16 [4096, 4096], P('tp'), may hold values from -0.125 to 0.125
Outputs:
- mixed: bfloat16 [8192, 4096], P('ctx', 'tp')
The draws below stay inside these ranges and needn't reach their ends.
Inputs may be any that keep to these rules, and one draw needn't show every extreme that they name: `rates`: each rate lies between 0.25 / 8192 and 1 / 32.
All inputs are finite; a program needn't handle non-finite values.
Results may differ from the reference program's by a relative error of at most 0.015.
Values may be sent and summed in bfloat16 or wider, within the bound.
A program may use at most 128 MiB of HBM per device.

```python
import math
import jax
import jax.numpy as jnp
from jax import lax

D = 4096
SHARE = 16
STATE = 16
GROUPS = 256
LENGTH = 8192


def draw_rates(key, part):
    seeded = jax.random.fold_in(key, 7)
    pick_key, slow_key, fast_key = jax.random.split(seeded, 3)
    grid_shape = (GROUPS, STATE)
    lowest = math.log(0.25 / LENGTH)
    highest = math.log(1.0 / 32.0)
    middle = min(math.log(2.0 / LENGTH), highest)
    portion = 0.5
    chosen = jax.random.uniform(pick_key, grid_shape, jnp.float32) < portion
    slow_log = jax.random.uniform(slow_key, grid_shape, jnp.float32, lowest, middle)
    fast_log = jax.random.uniform(fast_key, grid_shape, jnp.float32, middle, highest)
    return jnp.exp(jnp.where(chosen, slow_log, fast_log)).astype(jnp.float32)


def spiked(result, key, source, target, blocks, factor):
    owner, partner = [(jnp.arange(result.shape[axis_at]) // (result.shape[axis_at] // blocks)).reshape([-1 if axis == axis_at else 1 for axis in range(result.ndim)]) for axis_at in (source, target)]
    chosen = jax.random.permutation(key, blocks)[partner]
    strong = (owner == chosen) | (owner == (partner + blocks // 2) % blocks)
    return jnp.where(strong, factor * result, result)


def shard_levels(rng, extent, cuts, least, top_value):
    loudness = 1.0
    for dim, blocks in cuts:
        heights = jax.random.uniform(jax.random.fold_in(jax.random.fold_in(rng, 6), dim), (blocks,), jnp.float32, least / len(cuts), top_value / len(cuts))
        loudness = loudness * jnp.repeat(jnp.exp(heights), extent[dim] // blocks).reshape((-1,) + (1,) * (len(extent) - 1 - dim))
    return loudness


def scatter_about(rng, dims, spread, bound, shards=(), kind=jnp.bfloat16):
    result = jax.random.normal(rng, dims, jnp.float32) * spread
    if len(shards) > 0:
        result = shard_levels(rng, dims, shards, -0.22, 0.18) * result
    return jnp.clip(result, min=-bound, max=bound).astype(kind)


def noise_with(own_key, extent, deviation, limit, pieces, heavy, kind=jnp.bfloat16):
    values = deviation * jax.random.normal(own_key, extent, jnp.float32)
    if pieces:
        values = values * shard_levels(own_key, extent, pieces, -0.22, 0.18)
    return jnp.clip(spiked(values, jax.random.fold_in(own_key, 3), *heavy), -limit, limit).astype(kind)


def setup_inputs(seed: int = 0) -> dict:
    arg_keys = jax.random.split(jax.random.key(seed), 7)
    query = scatter_about(arg_keys[0], (LENGTH, D), 1.0, 6.0, ((0, 8), (1, 4)))
    keys = scatter_about(arg_keys[1], (LENGTH, D), 1.0, 6.0, ((0, 8), (1, 4)))
    values = scatter_about(arg_keys[2], (LENGTH, D), 1.0, 6.0, ((0, 8), (1, 4)))
    residues = scatter_about(arg_keys[3], (GROUPS, STATE), STATE ** -0.5, 1.5, (), jnp.float32)
    rates = draw_rates(jax.random.fold_in(arg_keys[6], 71), 0)
    w_out = noise_with(arg_keys[5], (D, D), D ** -0.5, 0.125, ((0, 4),), (0, 1, 4, 2.0))
    return {"query": query, "keys": keys, "values": values, "residues": residues, "rates": rates, "w_out": w_out}


def modal_filter(residues, rates, count):
    position = jnp.arange(count, dtype=jnp.float32)
    mode_gain = residues * jnp.sqrt(2.0 * rates)
    fading = jnp.exp(-rates[:, :, None] * position[None, None, :])
    return jnp.einsum('gs,gst->tg', mode_gain, fading)

def reference(query, keys, values, residues, rates, w_out):
    product = (keys.astype(jnp.float32) * values.astype(jnp.float32)).astype(jnp.bfloat16)
    product = lax.optimization_barrier(product)
    kernel = modal_filter(residues, rates, LENGTH)
    grouped = product.astype(jnp.float32).reshape(LENGTH, GROUPS, SHARE).transpose(1, 0, 2)

    def per_group(member):
        signal, taps = member
        padded = 2 * LENGTH
        spectrum = jnp.fft.rfft(signal, n=padded, axis=0) * jnp.fft.rfft(taps, n=padded)[:, None]
        return jnp.fft.irfft(spectrum, n=padded, axis=0)[:LENGTH]
    folded = lax.map(per_group, (grouped, kernel.T))
    convolved = folded.transpose(1, 0, 2).reshape(LENGTH, D).astype(jnp.bfloat16)
    convolved = lax.optimization_barrier(convolved)
    gated = (query.astype(jnp.float32) * convolved.astype(jnp.float32)).astype(jnp.bfloat16)
    return jnp.dot(gated, w_out, preferred_element_type=jnp.float32).astype(jnp.bfloat16)
```

```python
import functools
import math

import jax
import jax.numpy as jnp
from jax import lax
from jax.experimental import pallas as pl
from jax.experimental.pallas import tpu as pltpu
from jax.sharding import PartitionSpec as P

SHARE = 16
LANES = 128
MESH = pl.DeviceIdType.MESH
F32 = jnp.float32
BF16 = jnp.bfloat16


def split(x):
    upper = x.astype(BF16)
    return upper, (x - upper.astype(F32)).astype(BF16)


def dot(a, b):
    return jnp.dot(a, b, preferred_element_type=F32)


def conv_kernel(ctx, state, chunk, q_ref, k_ref, v_ref, rrow_ref, grow_ref, rcol_ref, rlane_ref, gmask_ref,
                smask_ref, out_ref, states, own, before, inside, wide, taps, carry, send_sem, recv_sem):
    block, width = q_ref.shape
    chunks = block // chunk
    lane_blocks = width // LANES
    groups = LANES // SHARE
    modes = groups * state
    me = lax.axis_index("ctx")

    barrier = pltpu.get_barrier_semaphore()

    def greet(d, _):
        pl.semaphore_signal(barrier, inc=1, device_id={"ctx": lax.rem(me + d, ctx)}, device_id_type=MESH)
        return 0

    lax.fori_loop(1, ctx, greet, 0)

    def product(k, lanes):
        rows = pl.ds(k * chunk, chunk)
        return (k_ref[rows, lanes].astype(F32) * v_ref[rows, lanes].astype(F32)).astype(BF16)

    def lanes_of(b):
        return pl.ds(pl.multiple_of(b * LANES, LANES), LANES)

    def rates_col(b):
        return rcol_ref[pl.ds(pl.multiple_of(b * modes, modes), modes), :]

    def state_step(b, _):
        lanes = lanes_of(b)
        tau = lax.broadcasted_iota(jnp.int32, (modes, chunk), 1).astype(F32)
        upper, lower = split(jnp.exp(-rates_col(b) * (chunk - 1.0 - tau)))
        decay = jnp.exp(-rlane_ref[:, lanes] * float(chunk))
        gmask = gmask_ref[...]
        total = jnp.zeros((state, LANES), F32)
        for k in range(chunks):
            x = product(k, lanes)
            fresh = (dot(upper, x) + dot(lower, x)) * gmask
            before[k, :, lanes] = total
            total = total * decay + fresh.reshape(groups, state, LANES).sum(0)
        own[:, lanes] = total
        return 0

    lax.fori_loop(0, lane_blocks, state_step, 0)

    pl.semaphore_wait(barrier, ctx - 1)

    def to_peer(d):
        return pltpu.make_async_remote_copy(
            src_ref=own, dst_ref=states.at[me], send_sem=send_sem.at[d], recv_sem=recv_sem.at[me],
            device_id={"ctx": lax.rem(me + d, ctx)}, device_id_type=MESH)

    def from_peer(j):
        return pltpu.make_async_remote_copy(
            src_ref=own, dst_ref=states.at[j], send_sem=send_sem.at[0], recv_sem=recv_sem.at[j],
            device_id={"ctx": j}, device_id_type=MESH)

    lax.fori_loop(1, ctx - me, lambda d, _: (to_peer(d).start(), 0)[1], 0)

    def inside_step(b, _):
        lanes = lanes_of(b)
        row = lax.broadcasted_iota(jnp.int32, (chunk, modes), 0).astype(F32)
        col = lax.broadcasted_iota(jnp.int32, (modes, chunk), 1).astype(F32)
        middle = chunk / 2.0
        falling = grow_ref[pl.ds(b, 1), :] * jnp.exp(-rrow_ref[pl.ds(b, 1), :] * (row - middle))
        b_hi, b_lo = split(jnp.exp(rates_col(b) * (col - middle)))
        causal = lax.broadcasted_iota(jnp.int32, (chunk, chunk), 0) >= lax.broadcasted_iota(
            jnp.int32, (chunk, chunk), 1)
        xs = [product(k, lanes) for k in range(chunks)]
        for g in range(groups):
            a_hi, a_lo = split(falling * smask_ref[g:g + 1, :])
            tap = dot(a_hi, b_hi) + dot(a_lo, b_hi) + dot(a_hi, b_lo)
            taps[:, g * chunk:(g + 1) * chunk] = jnp.where(causal, tap, 0.0).astype(BF16)
            only = gmask_ref[g * state:g * state + 1, :].astype(BF16)
            for k in range(chunks):
                wide[g * chunk:(g + 1) * chunk, k * LANES:(k + 1) * LANES] = xs[k] * only
        inside[b] = dot(taps[...], wide[...])
        return 0

    lax.fori_loop(0, lane_blocks, inside_step, 0)

    lax.fori_loop(0, me, lambda j, _: (from_peer(j).wait_recv(), 0)[1], 0)

    def carry_step(b, _):
        lanes = lanes_of(b)
        rlane = rlane_ref[:, lanes]
        hop = jnp.exp(-rlane * float(block))
        decay = jnp.exp(-rlane * float(chunk))
        reached = lax.fori_loop(
            0, me, lambda j, r: r * hop + states[j, :, lanes], jnp.zeros((state, LANES), F32))
        gmask = gmask_ref[...]
        for k in range(chunks):
            entering = before[k, :, lanes] + reached
            reached = reached * decay
            spread = jnp.concatenate([entering] * groups, axis=0) * gmask
            hi, lo = split(spread)
            at = slice(k * LANES, (k + 1) * LANES)
            carry[0:modes, at] = hi
            carry[modes:2 * modes, at] = hi
            carry[2 * modes:3 * modes, at] = lo
        row = lax.broadcasted_iota(jnp.int32, (chunk, modes), 0).astype(F32)
        hi, lo = split(grow_ref[pl.ds(b, 1), :] * jnp.exp(-rrow_ref[pl.ds(b, 1), :] * (row + 1.0)))
        full = inside[b] + dot(jnp.concatenate([hi, lo, hi], axis=1), carry[...])
        for k in range(chunks):
            rows = pl.ds(k * chunk, chunk)
            convolved = full[:, k * LANES:(k + 1) * LANES].astype(BF16)
            out_ref[rows, lanes] = (q_ref[rows, lanes].astype(F32) * convolved.astype(F32)).astype(BF16)
        return 0

    lax.fori_loop(0, lane_blocks, carry_step, 0)
    lax.fori_loop(1, ctx - me, lambda d, _: (to_peer(d).wait_send(), 0)[1], 0)


def gated_conv(query, keys, values, rates, gain, ctx):
    block, width = keys.shape
    state = rates.shape[1]
    chunk = math.gcd(block, LANES)
    chunks = block // chunk
    groups = LANES // SHARE
    modes = groups * state
    lane_blocks = width // LANES
    rows = jnp.arange(modes)[:, None] // state
    gmask = (rows == jnp.arange(LANES)[None, :] // SHARE).astype(F32)
    smask = (jnp.arange(groups)[:, None] == jnp.arange(modes)[None, :] // state).astype(F32)
    vmem = pl.BlockSpec(memory_space=pltpu.VMEM)
    return pl.pallas_call(
        functools.partial(conv_kernel, ctx, state, chunk),
        out_shape=jax.ShapeDtypeStruct((block, width), BF16),
        in_specs=[vmem] * 9,
        out_specs=vmem,
        scratch_shapes=[
            pltpu.VMEM((ctx, state, width), F32),
            pltpu.VMEM((state, width), F32),
            pltpu.VMEM((chunks, state, width), F32),
            pltpu.VMEM((lane_blocks, chunk, chunks * LANES), F32),
            pltpu.VMEM((groups * chunk, chunks * LANES), BF16),
            pltpu.VMEM((chunk, groups * chunk), BF16),
            pltpu.VMEM((3 * modes, chunks * LANES), BF16),
            pltpu.SemaphoreType.DMA((ctx,)),
            pltpu.SemaphoreType.DMA((ctx,)),
        ],
        compiler_params=pltpu.CompilerParams(
            collective_id=0, has_side_effects=True, vmem_limit_bytes=40 * 2**20),
        cost_estimate=pl.CostEstimate(
            flops=40 * block * width * chunk, bytes_accessed=8 * block * width, transcendentals=0),
        name="gated_conv",
    )(query, keys, values, rates.reshape(lane_blocks, modes), gain.reshape(lane_blocks, modes),
      rates.reshape(lane_blocks * modes, 1), jnp.repeat(rates.T, SHARE, axis=1), gmask, smask)


def on_device(ctx, tp, query, keys, values, residues, rates, w_out):
    width = keys.shape[1]
    groups = width // SHARE
    place = lax.axis_index("tp")
    rates = lax.dynamic_slice_in_dim(rates, place * groups, groups, 0)
    residues = lax.dynamic_slice_in_dim(residues, place * groups, groups, 0)
    gain = residues * jnp.sqrt(2.0 * rates)
    gated = gated_conv(query, keys, values, rates, gain, ctx)
    mixed = dot(gated, w_out).astype(BF16)
    return lax.psum_scatter(mixed, "tp", scatter_dimension=1, tiled=True)


def solution(mesh):
    in_specs = (P("ctx", "tp"), P("ctx", "tp"), P("ctx", "tp"), P(), P(), P("tp", None))
    return jax.shard_map(
        functools.partial(on_device, mesh.shape["ctx"], mesh.shape["tp"]),
        mesh=mesh, in_specs=in_specs, out_specs=P("ctx", "tp"), check_vma=False)
```

```python
import functools
import math

import jax
import jax.numpy as jnp
from jax import lax
from jax.experimental import pallas as pl
from jax.experimental.pallas import tpu as pltpu
from jax.sharding import PartitionSpec as P

SHARE = 16
LANES = 128
MESH = pl.DeviceIdType.MESH
F32 = jnp.float32
BF16 = jnp.bfloat16


def split(x):
    upper = x.astype(BF16)
    return upper, (x - upper.astype(F32)).astype(BF16)


def dot(a, b):
    return jnp.dot(a, b, preferred_element_type=F32)


def conv_kernel(ctx, state, chunk, q_ref, k_ref, v_ref, rrow_ref, grow_ref, rcol_ref, rlane_ref, gmask_ref,
                smask_ref, out_ref, states, own, before, inside, wide, taps, carry, send_sem, recv_sem):
    block, width = q_ref.shape
    chunks = block // chunk
    lane_blocks = width // LANES
    groups = LANES // SHARE
    modes = groups * state
    me = lax.axis_index("ctx")

    barrier = pltpu.get_barrier_semaphore()

    def greet(d, _):
        pl.semaphore_signal(barrier, inc=1, device_id={"ctx": lax.rem(me + d, ctx)}, device_id_type=MESH)
        return 0

    lax.fori_loop(1, ctx, greet, 0)

    def product(k, lanes):
        rows = pl.ds(k * chunk, chunk)
        return (k_ref[rows, lanes].astype(F32) * v_ref[rows, lanes].astype(F32)).astype(BF16)

    def lanes_of(b):
        return pl.ds(pl.multiple_of(b * LANES, LANES), LANES)

    def rates_col(b):
        return rcol_ref[pl.ds(pl.multiple_of(b * modes, modes), modes), :]

    def state_step(b, _):
        lanes = lanes_of(b)
        tau = lax.broadcasted_iota(jnp.int32, (modes, chunk), 1).astype(F32)
        upper, lower = split(jnp.exp(-rates_col(b) * (chunk - 1.0 - tau)))
        decay = jnp.exp(-rlane_ref[:, lanes] * float(chunk))
        gmask = gmask_ref[...]
        total = jnp.zeros((state, LANES), F32)
        for k in range(chunks):
            x = product(k, lanes)
            fresh = (dot(upper, x) + dot(lower, x)) * gmask
            before[k, :, lanes] = total
            total = total * decay + fresh.reshape(groups, state, LANES).sum(0)
        own[:, lanes] = total
        return 0

    lax.fori_loop(0, lane_blocks, state_step, 0)

    pl.semaphore_wait(barrier, ctx - 1)

    def to_peer(d):
        return pltpu.make_async_remote_copy(
            src_ref=own, dst_ref=states.at[me], send_sem=send_sem.at[d], recv_sem=recv_sem.at[me],
            device_id={"ctx": lax.rem(me + d, ctx)}, device_id_type=MESH)

    def from_peer(j):
        return pltpu.make_async_remote_copy(
            src_ref=own, dst_ref=states.at[j], send_sem=send_sem.at[0], recv_sem=recv_sem.at[j],
            device_id={"ctx": j}, device_id_type=MESH)

    lax.fori_loop(1, ctx - me, lambda d, _: (to_peer(d).start(), 0)[1], 0)

    def inside_step(b, _):
        lanes = lanes_of(b)
        row = lax.broadcasted_iota(jnp.int32, (chunk, modes), 0).astype(F32)
        col = lax.broadcasted_iota(jnp.int32, (modes, chunk), 1).astype(F32)
        middle = chunk / 2.0
        falling = grow_ref[pl.ds(b, 1), :] * jnp.exp(-rrow_ref[pl.ds(b, 1), :] * (row - middle))
        b_hi, b_lo = split(jnp.exp(rates_col(b) * (col - middle)))
        causal = lax.broadcasted_iota(jnp.int32, (chunk, chunk), 0) >= lax.broadcasted_iota(
            jnp.int32, (chunk, chunk), 1)
        xs = [product(k, lanes) for k in range(chunks)]
        for g in range(groups):
            a_hi, a_lo = split(falling * smask_ref[g:g + 1, :])
            tap = dot(a_hi, b_hi) + dot(a_lo, b_hi) + dot(a_hi, b_lo)
            taps[:, g * chunk:(g + 1) * chunk] = jnp.where(causal, tap, 0.0).astype(BF16)
            only = gmask_ref[g * state:g * state + 1, :].astype(BF16)
            for k in range(chunks):
                wide[g * chunk:(g + 1) * chunk, k * LANES:(k + 1) * LANES] = xs[k] * only
        inside[b] = dot(taps[...], wide[...])
        return 0

    lax.fori_loop(0, lane_blocks, inside_step, 0)

    lax.fori_loop(0, me, lambda j, _: (from_peer(j).wait_recv(), 0)[1], 0)

    def carry_step(b, _):
        lanes = lanes_of(b)
        rlane = rlane_ref[:, lanes]
        hop = jnp.exp(-rlane * float(block))
        decay = jnp.exp(-rlane * float(chunk))
        reached = lax.fori_loop(
            0, me, lambda j, r: r * hop + states[j, :, lanes], jnp.zeros((state, LANES), F32))
        gmask = gmask_ref[...]
        for k in range(chunks):
            entering = before[k, :, lanes] + reached
            reached = reached * decay
            spread = jnp.concatenate([entering] * groups, axis=0) * gmask
            hi, lo = split(spread)
            at = slice(k * LANES, (k + 1) * LANES)
            carry[0:modes, at] = hi
            carry[modes:2 * modes, at] = hi
            carry[2 * modes:3 * modes, at] = lo
        row = lax.broadcasted_iota(jnp.int32, (chunk, modes), 0).astype(F32)
        hi, lo = split(grow_ref[pl.ds(b, 1), :] * jnp.exp(-rrow_ref[pl.ds(b, 1), :] * (row + 1.0)))
        full = inside[b] + dot(jnp.concatenate([hi, lo, hi], axis=1), carry[...])
        for k in range(chunks):
            rows = pl.ds(k * chunk, chunk)
            convolved = full[:, k * LANES:(k + 1) * LANES].astype(BF16)
            out_ref[rows, lanes] = (q_ref[rows, lanes].astype(F32) * convolved.astype(F32)).astype(BF16)
        return 0

    lax.fori_loop(0, lane_blocks, carry_step, 0)
    lax.fori_loop(1, ctx - me, lambda d, _: (to_peer(d).wait_send(), 0)[1], 0)


def gated_conv(query, keys, values, rates, gain, ctx):
    block, width = keys.shape
    state = rates.shape[1]
    chunk = math.gcd(block, LANES)
    chunks = block // chunk
    groups = LANES // SHARE
    modes = groups * state
    lane_blocks = width // LANES
    rows = jnp.arange(modes)[:, None] // state
    gmask = (rows == jnp.arange(LANES)[None, :] // SHARE).astype(F32)
    smask = (jnp.arange(groups)[:, None] == jnp.arange(modes)[None, :] // state).astype(F32)
    vmem = pl.BlockSpec(memory_space=pltpu.VMEM)
    return pl.pallas_call(
        functools.partial(conv_kernel, ctx, state, chunk),
        out_shape=jax.ShapeDtypeStruct((block, width), BF16),
        in_specs=[vmem] * 9,
        out_specs=vmem,
        scratch_shapes=[
            pltpu.VMEM((ctx, state, width), F32),
            pltpu.VMEM((state, width), F32),
            pltpu.VMEM((chunks, state, width), F32),
            pltpu.VMEM((lane_blocks, chunk, chunks * LANES), F32),
            pltpu.VMEM((groups * chunk, chunks * LANES), BF16),
            pltpu.VMEM((chunk, groups * chunk), BF16),
            pltpu.VMEM((3 * modes, chunks * LANES), BF16),
            pltpu.SemaphoreType.DMA((ctx,)),
            pltpu.SemaphoreType.DMA((ctx,)),
        ],
        compiler_params=pltpu.CompilerParams(
            collective_id=0, has_side_effects=True, vmem_limit_bytes=40 * 2**20),
        cost_estimate=pl.CostEstimate(
            flops=40 * block * width * chunk, bytes_accessed=8 * block * width, transcendentals=0),
        name="gated_conv",
    )(query, keys, values, rates.reshape(lane_blocks, modes), gain.reshape(lane_blocks, modes),
      rates.reshape(lane_blocks * modes, 1), jnp.repeat(rates.T, SHARE, axis=1), gmask, smask)


def project_kernel(ctx, tp, tiles, gated_ref, w_hbm, *rest):
    slices = rest[:tp - 1]
    (out_ref, w_ref, columns, right_buf, left_buf, part, w_sem, own_sem, spread_send, spread_recv,
     right_send, right_recv, left_send, left_recv) = rest[tp - 1:]
    block, width = gated_ref.shape
    rows = block // (2 * tiles)
    piece = slices[0].shape[0]
    place = lax.axis_index("tp")
    far = tp - 1 - place
    me = lax.axis_index("ctx")
    has_left = place > 0
    has_right = place < tp - 1

    w_copy = pltpu.make_async_copy(w_hbm, w_ref, w_sem)
    w_copy.start()

    barrier = pltpu.get_barrier_semaphore()

    def greet(d, _):
        pl.semaphore_signal(barrier, inc=1, device_id={"ctx": lax.rem(me + d, ctx)}, device_id_type=MESH)
        return 0

    lax.fori_loop(1, ctx, greet, 0)

    @pl.when(has_left)
    def _():
        pl.semaphore_signal(barrier, inc=1, device_id={"tp": place - 1}, device_id_type=MESH)

    @pl.when(has_right)
    def _():
        pl.semaphore_signal(barrier, inc=1, device_id={"tp": place + 1}, device_id_type=MESH)

    pl.semaphore_wait(barrier, ctx - 1 + has_left.astype(jnp.int32) + has_right.astype(jnp.int32))

    def rightward(src, group, m):
        return pltpu.make_async_remote_copy(
            src_ref=src, dst_ref=right_buf.at[group, m], send_sem=right_send.at[group, m],
            recv_sem=right_recv.at[group, m], device_id={"tp": place + 1}, device_id_type=MESH)

    def leftward(src, group, m):
        return pltpu.make_async_remote_copy(
            src_ref=src, dst_ref=left_buf.at[group, m], send_sem=left_send.at[group, m],
            recv_sem=left_recv.at[group, m], device_id={"tp": place - 1}, device_id_type=MESH)

    def whole_tile(m):
        return pl.ds(pl.multiple_of(m * rows, rows), rows)

    def summed_tile(m):
        return pl.ds(pl.multiple_of((tiles + m) * rows, rows), rows)

    def share(m, dest):
        cols = pl.ds(pl.multiple_of(dest * width, width), width)
        return dot(gated_ref[summed_tile(m), :], w_ref[:, cols])

    def first_step(m, _):
        src = gated_ref.at[whole_tile(m)]

        @pl.when(has_right)
        def _():
            rightward(src, 0, m).start()

        @pl.when(has_left)
        def _():
            leftward(src, 0, m).start()
        return 0

    lax.fori_loop(0, tiles, first_step, 0)

    def spread(d, k):
        at = pl.ds(pl.multiple_of(me * piece, piece), piece)
        return pltpu.make_async_remote_copy(
            src_ref=slices[k], dst_ref=columns.at[k, at], send_sem=spread_send.at[d, k],
            recv_sem=spread_recv.at[me, k], device_id={"ctx": lax.rem(me + d, ctx)}, device_id_type=MESH)

    def gathered(d, k):
        peer = lax.rem(me + d, ctx)
        at = pl.ds(pl.multiple_of(peer * piece, piece), piece)
        return pltpu.make_async_remote_copy(
            src_ref=slices[k], dst_ref=columns.at[k, at], send_sem=spread_send.at[d, k],
            recv_sem=spread_recv.at[peer, k], device_id={"ctx": peer}, device_id_type=MESH)

    def kept(k):
        at = pl.ds(pl.multiple_of(me * piece, piece), piece)
        return pltpu.make_async_copy(slices[k], columns.at[k, at], own_sem.at[k])

    def spread_step(d, _):
        for k in range(tp - 1):
            spread(d, k).start()
        return 0

    lax.fori_loop(1, ctx, spread_step, 0)
    for k in range(tp - 1):
        kept(k).start()
    w_copy.wait()

    def forward(group, m, steps_in, from_there, to_there, buf, copy, dest):
        @pl.when(to_there & (group > steps_in))
        def _():
            part[...] = share(m, dest)

        @pl.when(from_there)
        def _():
            copy(buf.at[group - 1, m], group - 1, m).wait_recv()

        @pl.when(to_there & (group > steps_in) & from_there)
        def _():
            buf[group - 1, m] = (part[...] + buf[group - 1, m].astype(F32)).astype(BF16)

        @pl.when(to_there & (group > steps_in) & jnp.logical_not(from_there))
        def _():
            buf[group - 1, m] = part[...].astype(BF16)

        @pl.when(to_there)
        def _():
            copy(buf.at[group - 1, m], group, m).start()

    def step(t, _):
        group = t // tiles
        m = t % tiles
        forward(group, m, place, has_left, has_right, right_buf, rightward, tp + place - group)
        forward(group, m, far, has_right, has_left, left_buf, leftward, group - far - 1)
        return 0

    lax.fori_loop(tiles, tp * tiles, step, 0)

    def gathered_step(d, _):
        for k in range(tp - 1):
            gathered(d, k).wait_recv()
        return 0

    lax.fori_loop(1, ctx, gathered_step, 0)
    for k in range(tp - 1):
        kept(k).wait()

    own_cols = pl.ds(pl.multiple_of(place * width, width), width)

    def whole_step(m, _):
        part[...] = dot(gated_ref[whole_tile(m), :], w_ref[:, own_cols])

        def add_left(i, _):
            part[...] += dot(right_buf[i, m], columns[i])
            return 0

        def add_right(i, _):
            part[...] += dot(left_buf[i, m], columns[tp - 2 - i])
            return 0

        lax.fori_loop(0, place, add_left, 0)
        lax.fori_loop(0, far, add_right, 0)
        out_ref[whole_tile(m), :] = part[...].astype(BF16)
        return 0

    lax.fori_loop(0, tiles, whole_step, 0)

    def summed_step(m, _):
        part[...] = share(m, place)

        @pl.when(has_left)
        def _():
            rightward(right_buf.at[tp - 1, m], tp - 1, m).wait_recv()
            part[...] += right_buf[tp - 1, m].astype(F32)

        @pl.when(has_right)
        def _():
            leftward(left_buf.at[tp - 1, m], tp - 1, m).wait_recv()
            part[...] += left_buf[tp - 1, m].astype(F32)

        out_ref[summed_tile(m), :] = part[...].astype(BF16)
        return 0

    lax.fori_loop(0, tiles, summed_step, 0)

    def sent_step(t, _):
        group = t // tiles
        m = t % tiles

        @pl.when(has_right)
        def _():
            rightward(right_buf.at[group, m], group, m).wait_send()

        @pl.when(has_left)
        def _():
            leftward(left_buf.at[group, m], group, m).wait_send()
        return 0

    lax.fori_loop(0, tp * tiles, sent_step, 0)

    def spread_done(d, _):
        for k in range(tp - 1):
            spread(d, k).wait_send()
        return 0

    lax.fori_loop(1, ctx, spread_done, 0)


def project(gated, w_out, slices, ctx, tp, tiles):
    block, width = gated.shape
    rows = block // (2 * tiles)
    vmem = pl.BlockSpec(memory_space=pltpu.VMEM)
    return pl.pallas_call(
        functools.partial(project_kernel, ctx, tp, tiles),
        out_shape=jax.ShapeDtypeStruct((block, width), BF16),
        in_specs=[vmem, pl.BlockSpec(memory_space=pl.ANY)] + [vmem] * (tp - 1),
        out_specs=vmem,
        scratch_shapes=[
            pltpu.VMEM(w_out.shape, BF16),
            pltpu.VMEM((tp - 1, w_out.shape[0], width), BF16),
            pltpu.VMEM((tp, tiles, rows, width), BF16),
            pltpu.VMEM((tp, tiles, rows, width), BF16),
            pltpu.VMEM((rows, width), F32),
            pltpu.SemaphoreType.DMA,
            pltpu.SemaphoreType.DMA((tp - 1,)),
            pltpu.SemaphoreType.DMA((ctx, tp - 1)),
            pltpu.SemaphoreType.DMA((ctx, tp - 1)),
            pltpu.SemaphoreType.DMA((tp, tiles)),
            pltpu.SemaphoreType.DMA((tp, tiles)),
            pltpu.SemaphoreType.DMA((tp, tiles)),
            pltpu.SemaphoreType.DMA((tp, tiles)),
        ],
        compiler_params=pltpu.CompilerParams(
            collective_id=1, has_side_effects=True, vmem_limit_bytes=48 * 2**20),
        cost_estimate=pl.CostEstimate(
            flops=2 * block * width * width * tp, bytes_accessed=8 * block * width, transcendentals=0),
        name="project",
    )(gated, w_out, *slices)


def on_device(ctx, tp, query, keys, values, residues, rates, w_out):
    width = keys.shape[1]
    groups = width // SHARE
    place = lax.axis_index("tp")
    piece = w_out.shape[0] // ctx
    first = lax.axis_index("ctx") * piece
    slices = []
    for k in range(1, tp):
        to = lax.rem(place + k, tp)
        mine = lax.dynamic_slice(w_out, (first, to * width), (piece, width))
        slices.append(lax.ppermute(mine, "tp", [(i, (i + k) % tp) for i in range(tp)]))
    rates = lax.dynamic_slice_in_dim(rates, place * groups, groups, 0)
    residues = lax.dynamic_slice_in_dim(residues, place * groups, groups, 0)
    gain = residues * jnp.sqrt(2.0 * rates)
    gated = gated_conv(query, keys, values, rates, gain, ctx)
    return project(gated, w_out, slices, ctx, tp, 4)


def solution(mesh):
    in_specs = (P("ctx", "tp"), P("ctx", "tp"), P("ctx", "tp"), P(), P(), P("tp", None))
    return jax.shard_map(
        functools.partial(on_device, mesh.shape["ctx"], mesh.shape["tp"]),
        mesh=mesh, in_specs=in_specs, out_specs=P("ctx", "tp"), check_vma=False)
```

```python
import functools
import math

import jax
import jax.numpy as jnp
import numpy as np
from jax import lax
from jax.experimental import pallas as pl
from jax.experimental.pallas import tpu as pltpu
from jax.sharding import PartitionSpec as P

SHARE = 16
LANES = 128
MESH = pl.DeviceIdType.MESH
F32 = jnp.float32
BF16 = jnp.bfloat16


def split(x):
    upper = x.astype(BF16)
    return upper, (x - upper.astype(F32)).astype(BF16)


def dot(a, b):
    return jnp.dot(a, b, preferred_element_type=F32)


def layer_kernel(ctx, tp, tiles, state, chunk, q_hbm, k_hbm, v_hbm, w_hbm, rates_ref, residues_ref, gmask_ref,
                 smask_ref, out_ref, q_ref, k_ref, v_ref, w_ref, gated, states, own, before, inside, wide, taps,
                 carry, extra, right_buf, left_buf, stage, part, load_sem, state_send, state_recv, hop_send,
                 hop_recv, spread_send, spread_recv, right_send, right_recv, left_send, left_recv):
    block, width = out_ref.shape
    chunks = block // chunk
    half = chunks // 2
    lane_blocks = width // LANES
    groups = LANES // SHARE
    modes = groups * state
    rows = block // (2 * tiles)
    piece = width // ctx
    inner = tp - 2
    me = lax.axis_index("ctx")
    place = lax.axis_index("tp")
    far = tp - 1 - place
    has_left = place > 0
    has_right = far > 0
    is_helper = (place == 1) | (far == 1)

    loads = [pltpu.make_async_copy(src, dst, load_sem.at[i]) for i, (src, dst) in enumerate(
        [(k_hbm, k_ref), (v_hbm, v_ref), (q_hbm, q_ref), (w_hbm, w_ref)])]
    for load in loads:
        load.start()

    barrier = pltpu.get_barrier_semaphore()

    def greet(d, _):
        pl.semaphore_signal(barrier, inc=1, device_id={"ctx": lax.rem(me + d, ctx)}, device_id_type=MESH)
        return 0

    lax.fori_loop(1, ctx, greet, 0)

    @pl.when(has_left)
    def _():
        pl.semaphore_signal(barrier, inc=1, device_id={"tp": place - 1}, device_id_type=MESH)

    @pl.when(has_right)
    def _():
        pl.semaphore_signal(barrier, inc=1, device_id={"tp": place + 1}, device_id_type=MESH)

    pl.semaphore_wait(barrier, ctx - 1 + has_left.astype(jnp.int32) + has_right.astype(jnp.int32))

    def column_block(order, from_left):
        return jnp.where(from_left, tp - 2 - order, order)

    def piece_rows(j):
        return pl.ds(pl.multiple_of(j * piece, piece), piece)

    def hop(order, to_right):
        e = column_block(order, to_right)
        cols = pl.ds(pl.multiple_of(jnp.where(to_right, e + 1, e) * width, width), width)
        return pltpu.make_async_remote_copy(
            src_ref=w_hbm.at[piece_rows(me), cols], dst_ref=extra.at[e, piece_rows(me)],
            send_sem=hop_send.at[e], recv_sem=hop_recv.at[e],
            device_id={"tp": jnp.where(to_right, place + 1, place - 1)}, device_id_type=MESH)

    def hop_step(order, _):
        hop(order, place == 0).start()
        return 0

    @pl.when((place == 0) | (far == 0))
    def _():
        lax.fori_loop(0, tp - 1, hop_step, 0)

    def spread(order, d):
        e = column_block(order, place == 1)
        return pltpu.make_async_remote_copy(
            src_ref=extra.at[e, piece_rows(me)], dst_ref=extra.at[e, piece_rows(me)],
            send_sem=spread_send.at[e, d], recv_sem=spread_recv.at[e, me],
            device_id={"ctx": lax.rem(me + d, ctx)}, device_id_type=MESH)

    def gathered(order, d):
        e = column_block(order, place == 1)
        peer = lax.rem(me + d, ctx)
        return pltpu.make_async_remote_copy(
            src_ref=extra.at[e, piece_rows(peer)], dst_ref=extra.at[e, piece_rows(peer)],
            send_sem=spread_send.at[e, d], recv_sem=spread_recv.at[e, peer],
            device_id={"ctx": peer}, device_id_type=MESH)

    def spread_block(order):
        e = column_block(order, place == 1)
        pltpu.make_async_remote_copy(
            src_ref=w_hbm.at[piece_rows(me), pl.ds(0, width)], dst_ref=extra.at[e, piece_rows(me)],
            send_sem=hop_send.at[e], recv_sem=hop_recv.at[e],
            device_id={"tp": jnp.where(place == 1, place - 1, place + 1)}, device_id_type=MESH).wait_recv()
        lax.fori_loop(1, ctx, lambda d, _: (spread(order, d).start(), 0)[1], 0)

    def await_block(order):
        lax.fori_loop(1, ctx, lambda d, _: (gathered(order, d).wait_recv(), 0)[1], 0)

    def product(k, lanes):
        at = pl.ds(k * chunk, chunk)
        return (k_ref[at, lanes].astype(F32) * v_ref[at, lanes].astype(F32)).astype(BF16)

    def lanes_of(b):
        return pl.ds(pl.multiple_of(b * LANES, LANES), LANES)

    def rate_row(b):
        return rates_ref[pl.ds(place * lane_blocks + b, 1), :]

    def gain_row(b):
        return residues_ref[pl.ds(place * lane_blocks + b, 1), :] * jnp.sqrt(2.0 * rate_row(b))

    def rate_columns(b):
        return jnp.broadcast_to(rate_row(b), (LANES, modes)).T

    def rate_lanes(b):
        return (rate_columns(b) * gmask_ref[...]).reshape(groups, state, LANES).sum(0)

    def state_step(b, _):
        lanes = lanes_of(b)
        tau = lax.broadcasted_iota(jnp.int32, (modes, chunk), 1).astype(F32)
        upper, lower = split(jnp.exp(-rate_columns(b) * (chunk - 1.0 - tau)))
        decay = jnp.exp(-rate_lanes(b) * float(chunk))
        gmask = gmask_ref[...]
        total = jnp.zeros((state, LANES), F32)
        for k in range(chunks):
            x = product(k, lanes)
            fresh = (dot(upper, x) + dot(lower, x)) * gmask
            before[k, :, lanes] = total
            total = total * decay + fresh.reshape(groups, state, LANES).sum(0)
        own[:, lanes] = total
        return 0

    loads[0].wait()
    loads[1].wait()
    lax.fori_loop(0, lane_blocks, state_step, 0)

    def to_peer(d):
        return pltpu.make_async_remote_copy(
            src_ref=own, dst_ref=states.at[me], send_sem=state_send.at[d], recv_sem=state_recv.at[me],
            device_id={"ctx": lax.rem(me + d, ctx)}, device_id_type=MESH)

    def from_peer(j):
        return pltpu.make_async_remote_copy(
            src_ref=own, dst_ref=states.at[j], send_sem=state_send.at[0], recv_sem=state_recv.at[j],
            device_id={"ctx": j}, device_id_type=MESH)

    lax.fori_loop(1, ctx - me, lambda d, _: (to_peer(d).start(), 0)[1], 0)

    def taps_step(b):
        row = lax.broadcasted_iota(jnp.int32, (chunk, modes), 0).astype(F32)
        col = lax.broadcasted_iota(jnp.int32, (modes, chunk), 1).astype(F32)
        middle = chunk / 2.0
        falling = gain_row(b) * jnp.exp(-rate_row(b) * (row - middle))
        b_hi, b_lo = split(jnp.exp(rate_columns(b) * (col - middle)))
        causal = lax.broadcasted_iota(jnp.int32, (chunk, chunk), 0) >= lax.broadcasted_iota(
            jnp.int32, (chunk, chunk), 1)
        for g in range(groups):
            a_hi, a_lo = split(falling * smask_ref[g:g + 1, :])
            tap = dot(a_hi, b_hi) + dot(a_lo, b_hi) + dot(a_hi, b_lo)
            taps[b, :, g * chunk:(g + 1) * chunk] = jnp.where(causal, tap, 0.0).astype(BF16)

    def inside_step(b, first):
        lanes = lanes_of(b)
        xs = [product(first + k, lanes) for k in range(half)]
        for g in range(groups):
            only = gmask_ref[g * state:g * state + 1, :].astype(BF16)
            for k in range(half):
                wide[g * chunk:(g + 1) * chunk, k * LANES:(k + 1) * LANES] = xs[k] * only
        inside[b] = dot(taps[b], wide[...])

    def carry_step(b, first):
        lanes = lanes_of(b)
        rlane = rate_lanes(b)
        along = jnp.exp(-rlane * float(block))
        decay = jnp.exp(-rlane * float(chunk))
        reached = lax.fori_loop(
            0, me, lambda j, r: r * along + states[j, :, lanes], jnp.zeros((state, LANES), F32))
        reached = reached * jnp.exp(-rlane * float(chunk * first))
        gmask = gmask_ref[...]
        for k in range(half):
            entering = before[first + k, :, lanes] + reached
            reached = reached * decay
            hi, lo = split(jnp.concatenate([entering] * groups, axis=0) * gmask)
            at = slice(k * LANES, (k + 1) * LANES)
            carry[0:modes, at] = hi
            carry[modes:2 * modes, at] = hi
            carry[2 * modes:3 * modes, at] = lo
        row = lax.broadcasted_iota(jnp.int32, (chunk, modes), 0).astype(F32)
        hi, lo = split(gain_row(b) * jnp.exp(-rate_row(b) * (row + 1.0)))
        full = inside[b] + dot(jnp.concatenate([hi, lo, hi], axis=1), carry[...])
        for k in range(half):
            at = pl.ds((first + k) * chunk, chunk)
            convolved = full[:, k * LANES:(k + 1) * LANES].astype(BF16)
            gated[at, lanes] = (q_ref[at, lanes].astype(F32) * convolved.astype(F32)).astype(BF16)

    def early_inside(b, _):
        taps_step(b)
        inside_step(b, 0)
        return 0

    def early_carry(b, _):
        carry_step(b, 0)
        return 0

    def late_step(b, _):
        inside_step(b, half)
        carry_step(b, half)
        return 0

    lax.fori_loop(0, lane_blocks, early_inside, 0)
    lax.fori_loop(0, me, lambda j, _: (from_peer(j).wait_recv(), 0)[1], 0)
    loads[2].wait()
    lax.fori_loop(0, lane_blocks, early_carry, 0)
    loads[3].wait()

    def early_tile(m):
        return pl.ds(pl.multiple_of(m * rows, rows), rows)

    def late_tile(m):
        return pl.ds(pl.multiple_of((tiles + m) * rows, rows), rows)

    def share(tile, dest):
        cols = pl.ds(pl.multiple_of(dest * width, width), width)
        return dot(gated[tile, :], w_ref[:, cols])

    def rightward(src, h, i, m):
        return pltpu.make_async_remote_copy(
            src_ref=src, dst_ref=right_buf.at[h, i, m], send_sem=right_send.at[h, i, m],
            recv_sem=right_recv.at[h, i, m], device_id={"tp": place + 1}, device_id_type=MESH)

    def leftward(src, h, i, m):
        return pltpu.make_async_remote_copy(
            src_ref=src, dst_ref=left_buf.at[h, i, m], send_sem=left_send.at[h, i, m],
            recv_sem=left_recv.at[h, i, m], device_id={"tp": place - 1}, device_id_type=MESH)

    flows = ((place, rightward, right_buf, lambda d: d), (far, leftward, left_buf, lambda d: tp - 1 - d))

    def sums_step(flow, h, i, m, tile, go):
        role, copy, buf, physical = flow
        came = i - (role >= 2).astype(jnp.int32)
        dest = tp - 1 - i + jnp.maximum(role - 1, 0)

        @pl.when(go)
        def _():
            part[...] = share(tile, physical(dest))

        @pl.when(go & (role > 0))
        def _():
            copy(buf.at[h, came, m], h, came, m).wait_recv()
            buf[h, came, m] = (part[...] + buf[h, came, m].astype(F32)).astype(BF16)

        @pl.when(go & (role == 0))
        def _():
            buf[h, came, m] = part[...].astype(BF16)

        @pl.when(go)
        def _():
            copy(buf.at[h, came, m], h, i, m).start()

    def early_step(t, _):
        i = t // tiles
        m = t % tiles
        for flow in flows:
            sums_step(flow, 0, i, m, early_tile(m), i >= flow[0] - 1)

        @pl.when(is_helper & (t < tp - 1))
        def _():
            spread_block(t)

        @pl.when(t < lane_blocks)
        def _():
            late_step(t, 0)
        return 0

    steps = inner * tiles
    lax.fori_loop(0, steps, early_step, 0)
    lax.fori_loop(steps, max(steps, lane_blocks), late_step, 0)

    def end_step(flow, i, m):
        role, copy, buf, physical = flow

        @pl.when((role == 0) & (i == 0))
        def _():
            copy(gated.at[late_tile(m)], 1, 0, m).start()

        @pl.when((role == 0) & (i == 1))
        def _():
            buf[1, 1, m] = share(early_tile(m), physical(1)).astype(BF16)
            copy(buf.at[1, 1, m], 1, 1, m).start()

    def helper_step(flow, i, m):
        role, copy, buf, physical = flow

        @pl.when(role == 1)
        def _():
            part[...] = share(late_tile(m), physical(tp - 1 - i))

            @pl.when(i == 0)
            def _():
                copy(buf.at[1, 0, m], 1, 0, m).wait_recv()

            @pl.when(m == 0)
            def _():
                await_block(i)

            stage[i, m] = (part[...] + dot(buf[1, 0, m], extra[column_block(i, place == 1)])).astype(BF16)
            copy(stage.at[i, m], 1, i, m).start()

    def late_sums(t, _):
        i = t // tiles
        m = t % tiles
        for flow in flows:
            end_step(flow, i, m)
            helper_step(flow, i, m)
            sums_step(flow, 1, i, m, late_tile(m), (flow[0] >= 2) & (i >= flow[0] - 1))
        return 0

    lax.fori_loop(0, steps, late_sums, 0)

    @pl.when(is_helper)
    def _():
        await_block(tp - 2)

    def last_step(m, _):
        part[...] = share(late_tile(m), place)
        for role, copy, buf, _physical in flows:
            @pl.when(role == 1)
            def _():
                part[...] += dot(buf[1, 0, m], extra[column_block(tp - 2, place == 1)])

            @pl.when(role >= 2)
            def _():
                copy(buf.at[1, inner - 1, m], 1, inner - 1, m).wait_recv()
                part[...] += buf[1, inner - 1, m].astype(F32)

        out_ref[late_tile(m), :] = part[...].astype(BF16)
        part[...] = share(early_tile(m), place)
        for role, copy, buf, _physical in flows:
            @pl.when(role == 1)
            def _():
                copy(buf.at[1, 1, m], 1, 1, m).wait_recv()
                part[...] += buf[1, 1, m].astype(F32)

            @pl.when(role >= 2)
            def _():
                copy(buf.at[0, inner - 1, m], 0, inner - 1, m).wait_recv()
                part[...] += buf[0, inner - 1, m].astype(F32)

        out_ref[early_tile(m), :] = part[...].astype(BF16)
        return 0

    lax.fori_loop(0, tiles, last_step, 0)

    def sent_step(t, _):
        i = t // tiles
        m = t % tiles
        for role, copy, buf, _physical in flows:
            for h in range(2):
                early_end = (role == 0) if h == 0 else (role == 0) & (i < 2)

                @pl.when(early_end | ((role > 0) & (i >= role - 1)))
                def _():
                    copy(buf.at[h, i, m], h, i, m).wait_send()
        return 0

    lax.fori_loop(0, steps, sent_step, 0)
    lax.fori_loop(1, ctx - me, lambda d, _: (to_peer(d).wait_send(), 0)[1], 0)

    @pl.when((place == 0) | (far == 0))
    def _():
        lax.fori_loop(0, tp - 1, lambda o, _: (hop(o, place == 0).wait_send(), 0)[1], 0)

    @pl.when(is_helper)
    def _():
        for order in range(tp - 1):
            lax.fori_loop(1, ctx, lambda d, _: (spread(order, d).wait_send(), 0)[1], 0)


def on_device(ctx, tp, query, keys, values, residues, rates, w_out):
    block, width = keys.shape
    state = rates.shape[1]
    chunk = math.gcd(block, LANES)
    chunks = block // chunk
    half = chunks // 2
    groups = LANES // SHARE
    modes = groups * state
    lane_blocks = width // LANES
    tiles = 4
    inner = tp - 2
    rows = block // (2 * tiles)
    at_row = np.arange(modes) // state
    gmask = jnp.asarray((at_row[:, None] == np.arange(LANES)[None, :] // SHARE).astype(np.float32))
    smask = jnp.asarray((np.arange(groups)[:, None] == at_row[None, :]).astype(np.float32))
    vmem = pl.BlockSpec(memory_space=pltpu.VMEM)
    hbm = pl.BlockSpec(memory_space=pl.ANY)
    dma = pltpu.SemaphoreType.DMA
    return pl.pallas_call(
        functools.partial(layer_kernel, ctx, tp, tiles, state, chunk),
        out_shape=jax.ShapeDtypeStruct((block, width), BF16),
        in_specs=[hbm] * 4 + [vmem] * 4,
        out_specs=vmem,
        scratch_shapes=[
            pltpu.VMEM((block, width), BF16),
            pltpu.VMEM((block, width), BF16),
            pltpu.VMEM((block, width), BF16),
            pltpu.VMEM(w_out.shape, BF16),
            pltpu.VMEM((block, width), BF16),
            pltpu.VMEM((ctx, state, width), F32),
            pltpu.VMEM((state, width), F32),
            pltpu.VMEM((chunks, state, width), F32),
            pltpu.VMEM((lane_blocks, chunk, half * LANES), F32),
            pltpu.VMEM((groups * chunk, half * LANES), BF16),
            pltpu.VMEM((lane_blocks, chunk, groups * chunk), BF16),
            pltpu.VMEM((3 * modes, half * LANES), BF16),
            pltpu.VMEM((tp - 1, width, width), BF16),
            pltpu.VMEM((2, inner, tiles, rows, width), BF16),
            pltpu.VMEM((2, inner, tiles, rows, width), BF16),
            pltpu.VMEM((inner, tiles, rows, width), BF16),
            pltpu.VMEM((rows, width), F32),
            dma((4,)),
            dma((ctx,)),
            dma((ctx,)),
            dma((tp - 1,)),
            dma((tp - 1,)),
            dma((tp - 1, ctx)),
            dma((tp - 1, ctx)),
            dma((2, inner, tiles)),
            dma((2, inner, tiles)),
            dma((2, inner, tiles)),
            dma((2, inner, tiles)),
        ],
        compiler_params=pltpu.CompilerParams(
            collective_id=0, has_side_effects=True, vmem_limit_bytes=56 * 2**20),
        cost_estimate=pl.CostEstimate(
            flops=4 * block * width * width * tp, bytes_accessed=24 * block * width, transcendentals=0),
        name="hyena_layer",
    )(query, keys, values, w_out, rates.reshape(-1, modes), residues.reshape(-1, modes), gmask, smask)


def solution(mesh):
    in_specs = (P("ctx", "tp"), P("ctx", "tp"), P("ctx", "tp"), P(), P(), P("tp", None))
    return jax.shard_map(
        functools.partial(on_device, mesh.shape["ctx"], mesh.shape["tp"]),
        mesh=mesh, in_specs=in_specs, out_specs=P("ctx", "tp"), check_vma=False)
```

```python
import functools
import math

import jax
import jax.numpy as jnp
import numpy as np
from jax import lax
from jax.experimental import pallas as pl
from jax.experimental.pallas import tpu as pltpu
from jax.sharding import PartitionSpec as P

SHARE = 16
LANES = 128
MESH = pl.DeviceIdType.MESH
F32 = jnp.float32
BF16 = jnp.bfloat16


def split(x):
    upper = x.astype(BF16)
    return upper, (x - upper.astype(F32)).astype(BF16)


def dot(a, b):
    return jnp.dot(a, b, preferred_element_type=F32)


def layer_kernel(ctx, tp, tiles, state, chunk, q_hbm, k_hbm, v_hbm, w_hbm, rates_ref, residues_ref, gmask_ref,
                 smask_ref, out_ref, q_ref, k_ref, v_ref, w_ref, columns, rate_rows, gain_rows, gated, states, own, before,
                 inside, wide, taps, carry, extra, right_buf, left_buf, stage, part, load_sem, state_send, state_recv, hop_send,
                 hop_recv, spread_send, spread_recv, right_send, right_recv, left_send, left_recv):
    block, width = out_ref.shape
    chunks = block // chunk
    half = chunks // 2
    lane_blocks = width // LANES
    groups = LANES // SHARE
    modes = groups * state
    rows = block // (2 * tiles)
    piece = width // ctx
    inner = tp - 2
    me = lax.axis_index("ctx")
    place = lax.axis_index("tp")
    far = tp - 1 - place
    has_left = place > 0
    has_right = far > 0
    is_helper = (place == 1) | (far == 1)

    loads = [pltpu.make_async_copy(src, dst, load_sem.at[i]) for i, (src, dst) in enumerate(
        [(k_hbm, k_ref), (v_hbm, v_ref), (q_hbm, q_ref), (w_hbm, w_ref)])]
    loads[0].start()
    loads[1].start()

    barrier = pltpu.get_barrier_semaphore()

    def greet(d, _):
        pl.semaphore_signal(barrier, inc=1, device_id={"ctx": lax.rem(me + d, ctx)}, device_id_type=MESH)
        return 0

    lax.fori_loop(1, ctx, greet, 0)

    @pl.when(has_left)
    def _():
        pl.semaphore_signal(barrier, inc=1, device_id={"tp": place - 1}, device_id_type=MESH)

    @pl.when(has_right)
    def _():
        pl.semaphore_signal(barrier, inc=1, device_id={"tp": place + 1}, device_id_type=MESH)

    pl.semaphore_wait(barrier, ctx - 1 + has_left.astype(jnp.int32) + has_right.astype(jnp.int32))

    def column_block(order, from_left):
        return jnp.where(from_left, tp - 2 - order, order)

    def piece_rows(j):
        return pl.ds(pl.multiple_of(j * piece, piece), piece)

    def hop(order, to_right):
        e = column_block(order, to_right)
        cols = pl.ds(pl.multiple_of(jnp.where(to_right, e + 1, e) * width, width), width)
        return pltpu.make_async_remote_copy(
            src_ref=w_hbm.at[piece_rows(me), cols], dst_ref=extra.at[e, piece_rows(me)],
            send_sem=hop_send.at[e], recv_sem=hop_recv.at[e],
            device_id={"tp": jnp.where(to_right, place + 1, place - 1)}, device_id_type=MESH)

    def hop_step(order, _):
        hop(order, place == 0).start()
        return 0

    @pl.when((place == 0) | (far == 0))
    def _():
        lax.fori_loop(0, tp - 1, hop_step, 0)

    chips = ctx // 2
    sibling = me + 1 - 2 * lax.rem(me, 2)

    def chip_peer(d):
        return lax.rem(me + 2 * d, ctx)

    def carried(order, j, send, peer):
        e = column_block(order, place == 1)
        return pltpu.make_async_remote_copy(
            src_ref=extra.at[e, piece_rows(j)], dst_ref=extra.at[e, piece_rows(j)],
            send_sem=spread_send.at[e, send], recv_sem=spread_recv.at[e, j],
            device_id={"ctx": peer}, device_id_type=MESH)

    def across(order, d):
        return carried(order, me, d, chip_peer(d))

    def beside(order, d):
        return carried(order, chip_peer(d), chips + d, sibling)

    def spread_block(order):
        e = column_block(order, place == 1)
        pltpu.make_async_remote_copy(
            src_ref=w_hbm.at[piece_rows(me), pl.ds(0, width)], dst_ref=extra.at[e, piece_rows(me)],
            send_sem=hop_send.at[e], recv_sem=hop_recv.at[e],
            device_id={"tp": jnp.where(place == 1, place - 1, place + 1)}, device_id_type=MESH).wait_recv()
        lax.fori_loop(1, chips, lambda d, _: (across(order, d).start(), 0)[1], 0)
        beside(order, 0).start()

    def relay_block(order):
        def relay(d, _):
            carried(order, chip_peer(d), d, chip_peer(d)).wait_recv()
            beside(order, d).start()
            return 0

        lax.fori_loop(1, chips, relay, 0)

    def await_block(order):
        def arrived(d, _):
            j = lax.rem(sibling + 2 * d, ctx)
            carried(order, j, chips + d, sibling).wait_recv()
            return 0

        lax.fori_loop(0, chips, arrived, 0)

    def product(k, lanes):
        at = pl.ds(k * chunk, chunk)
        return (k_ref[at, lanes].astype(F32) * v_ref[at, lanes].astype(F32)).astype(BF16)

    def lanes_of(b):
        return pl.ds(pl.multiple_of(b * LANES, LANES), LANES)

    def spread_rows(ref, b):
        every = ref.shape[1]
        tall = jnp.concatenate([ref[...]] * groups, axis=0)
        lane = lax.broadcasted_iota(jnp.int32, (groups, state, every), 2)
        group = lax.broadcasted_iota(jnp.int32, (groups, state, every), 0)
        first = (place * lane_blocks + b) * groups
        chosen = jnp.where(lane == group + first, tall.reshape(groups, state, every), 0.0)
        column = chosen.sum(axis=2, keepdims=True).reshape(modes, 1)
        return jnp.broadcast_to(column, (modes, LANES))

    def table_step(b, _):
        rate = spread_rows(rates_ref, b)
        columns[b] = rate
        rate_rows[b] = rate.T[0:8, :]
        gain_rows[b] = (spread_rows(residues_ref, b) * jnp.sqrt(2.0 * rate)).T[0:8, :]
        return 0

    def rate_row(b):
        return rate_rows[b, 0:1, :]

    def gain_row(b):
        return gain_rows[b, 0:1, :]

    def rate_columns(b):
        return columns[b]

    def rate_lanes(b):
        return (rate_columns(b) * gmask_ref[...]).reshape(groups, state, LANES).sum(0)

    def state_step(b, _):
        lanes = lanes_of(b)
        tau = lax.broadcasted_iota(jnp.int32, (modes, chunk), 1).astype(F32)
        fading = jnp.concatenate(split(jnp.exp(-rate_columns(b) * (chunk - 1.0 - tau))), axis=0)
        decay = jnp.exp(-rate_lanes(b) * float(chunk))
        gmask = gmask_ref[...]
        fresh = dot(fading, jnp.concatenate([product(k, lanes) for k in range(chunks)], axis=1))
        fresh = fresh[:modes] + fresh[modes:]
        total = jnp.zeros((state, LANES), F32)
        for k in range(chunks):
            before[k, :, lanes] = total
            new = fresh[:, k * LANES:(k + 1) * LANES] * gmask
            total = total * decay + new.reshape(groups, state, LANES).sum(0)
        own[:, lanes] = total
        return 0


    def to_peer(d):
        return pltpu.make_async_remote_copy(
            src_ref=own, dst_ref=states.at[me], send_sem=state_send.at[d], recv_sem=state_recv.at[me],
            device_id={"ctx": lax.rem(me + d, ctx)}, device_id_type=MESH)

    def from_peer(j):
        return pltpu.make_async_remote_copy(
            src_ref=own, dst_ref=states.at[j], send_sem=state_send.at[0], recv_sem=state_recv.at[j],
            device_id={"ctx": j}, device_id_type=MESH)

    def taps_step(b, _):
        row = lax.broadcasted_iota(jnp.int32, (chunk, modes), 0).astype(F32)
        col = lax.broadcasted_iota(jnp.int32, (modes, chunk), 1).astype(F32)
        middle = chunk / 2.0
        falling = gain_row(b) * jnp.exp(-rate_row(b) * (row - middle))
        b_hi, b_lo = split(jnp.exp(rate_columns(b) * (col - middle)))
        causal = lax.broadcasted_iota(jnp.int32, (chunk, chunk), 0) >= lax.broadcasted_iota(
            jnp.int32, (chunk, chunk), 1)
        a_hi, a_lo = split(jnp.concatenate([falling * smask_ref[g:g + 1, :] for g in range(groups)], axis=0))
        tap = dot(jnp.concatenate([a_hi, a_lo, a_hi], axis=1), jnp.concatenate([b_hi, b_hi, b_lo], axis=0))
        for g in range(groups):
            own_tap = jnp.where(causal, tap[g * chunk:(g + 1) * chunk], 0.0)
            taps[b, :, g * chunk:(g + 1) * chunk] = own_tap.astype(BF16)
        return 0

    def inside_step(b, first):
        lanes = lanes_of(b)
        xs = [product(first + k, lanes) for k in range(half)]
        for g in range(groups):
            only = gmask_ref[g * state:g * state + 1, :].astype(BF16)
            for k in range(half):
                wide[g * chunk:(g + 1) * chunk, k * LANES:(k + 1) * LANES] = xs[k] * only
        inside[b] = dot(taps[b], wide[...])

    def carry_step(b, first):
        lanes = lanes_of(b)
        rlane = rate_lanes(b)
        along = jnp.exp(-rlane * float(block))
        decay = jnp.exp(-rlane * float(chunk))
        reached = lax.fori_loop(
            0, me, lambda j, r: r * along + states[j, :, lanes], jnp.zeros((state, LANES), F32))
        reached = reached * jnp.exp(-rlane * float(chunk * first))
        gmask = gmask_ref[...]
        for k in range(half):
            entering = before[first + k, :, lanes] + reached
            reached = reached * decay
            hi, lo = split(jnp.concatenate([entering] * groups, axis=0) * gmask)
            at = slice(k * LANES, (k + 1) * LANES)
            carry[0:modes, at] = hi
            carry[modes:2 * modes, at] = hi
            carry[2 * modes:3 * modes, at] = lo
        row = lax.broadcasted_iota(jnp.int32, (chunk, modes), 0).astype(F32)
        hi, lo = split(gain_row(b) * jnp.exp(-rate_row(b) * (row + 1.0)))
        full = inside[b] + dot(jnp.concatenate([hi, lo, hi], axis=1), carry[...])
        for k in range(half):
            at = pl.ds((first + k) * chunk, chunk)
            convolved = full[:, k * LANES:(k + 1) * LANES].astype(BF16)
            gated[at, lanes] = (q_ref[at, lanes].astype(F32) * convolved.astype(F32)).astype(BF16)

    def early_inside(b, _):
        inside_step(b, 0)
        return 0

    def early_carry(b, _):
        carry_step(b, 0)
        return 0

    def late_step(b, _):
        inside_step(b, half)
        carry_step(b, half)
        return 0

    lax.fori_loop(0, lane_blocks, table_step, 0)
    lax.fori_loop(0, lane_blocks, taps_step, 0)
    loads[0].wait()
    loads[1].wait()
    loads[2].start()
    loads[3].start()
    lax.fori_loop(0, lane_blocks, state_step, 0)
    lax.fori_loop(1, ctx - me, lambda d, _: (to_peer(d).start(), 0)[1], 0)
    lax.fori_loop(0, lane_blocks, early_inside, 0)
    lax.fori_loop(0, me, lambda j, _: (from_peer(j).wait_recv(), 0)[1], 0)
    loads[2].wait()
    lax.fori_loop(0, lane_blocks, early_carry, 0)
    loads[3].wait()

    def early_tile(m):
        return pl.ds(pl.multiple_of(m * rows, rows), rows)

    def late_tile(m):
        return pl.ds(pl.multiple_of((tiles + m) * rows, rows), rows)

    def share(tile, dest):
        cols = pl.ds(pl.multiple_of(dest * width, width), width)
        return dot(gated[tile, :], w_ref[:, cols])

    def rightward(src, h, i, m):
        return pltpu.make_async_remote_copy(
            src_ref=src, dst_ref=right_buf.at[h, i, m], send_sem=right_send.at[h, i, m],
            recv_sem=right_recv.at[h, i, m], device_id={"tp": place + 1}, device_id_type=MESH)

    def leftward(src, h, i, m):
        return pltpu.make_async_remote_copy(
            src_ref=src, dst_ref=left_buf.at[h, i, m], send_sem=left_send.at[h, i, m],
            recv_sem=left_recv.at[h, i, m], device_id={"tp": place - 1}, device_id_type=MESH)

    flows = ((place, rightward, right_buf, lambda d: d), (far, leftward, left_buf, lambda d: tp - 1 - d))

    def sums_step(flow, h, i, m, tile, go):
        role, copy, buf, physical = flow
        came = i - (role >= 2).astype(jnp.int32)
        dest = tp - 1 - i + jnp.maximum(role - 1, 0)

        @pl.when(go)
        def _():
            part[...] = share(tile, physical(dest))

        @pl.when(go & (role > 0))
        def _():
            copy(buf.at[h, came, m], h, came, m).wait_recv()
            buf[h, came, m] = (part[...] + buf[h, came, m].astype(F32)).astype(BF16)

        @pl.when(go & (role == 0))
        def _():
            buf[h, came, m] = part[...].astype(BF16)

        @pl.when(go)
        def _():
            copy(buf.at[h, came, m], h, i, m).start()

    steps = inner * tiles

    def early_step(t, _):
        i = t // tiles
        m = t % tiles
        for flow in flows:
            sums_step(flow, 0, i, m, early_tile(m), i >= flow[0] - 1)

        @pl.when(is_helper & (t < tp - 1))
        def _():
            spread_block(t)

        @pl.when(is_helper & (t >= steps - (tp - 1)))
        def _():
            relay_block(t - (steps - (tp - 1)))

        @pl.when(t < lane_blocks)
        def _():
            late_step(t, 0)
        return 0

    lax.fori_loop(0, steps, early_step, 0)
    lax.fori_loop(steps, max(steps, lane_blocks), late_step, 0)

    def end_step(flow, i, m):
        role, copy, buf, physical = flow

        @pl.when((role == 0) & (i == 0))
        def _():
            copy(gated.at[late_tile(m)], 1, 0, m).start()

        @pl.when((role == 0) & (i == 1))
        def _():
            buf[1, 1, m] = share(early_tile(m), physical(1)).astype(BF16)
            copy(buf.at[1, 1, m], 1, 1, m).start()

    def helper_step(flow, i, m):
        role, copy, buf, physical = flow

        @pl.when(role == 1)
        def _():
            part[...] = share(late_tile(m), physical(tp - 1 - i))

            @pl.when(i == 0)
            def _():
                copy(buf.at[1, 0, m], 1, 0, m).wait_recv()

            @pl.when(m == 0)
            def _():
                await_block(i)

            stage[i, m] = (part[...] + dot(buf[1, 0, m], extra[column_block(i, place == 1)])).astype(BF16)
            copy(stage.at[i, m], 1, i, m).start()

    def late_sums(t, _):
        i = t // tiles
        m = t % tiles
        for flow in flows:
            end_step(flow, i, m)
            helper_step(flow, i, m)
            sums_step(flow, 1, i, m, late_tile(m), (flow[0] >= 2) & (i >= flow[0] - 1))
        return 0

    lax.fori_loop(0, steps, late_sums, 0)

    @pl.when(is_helper)
    def _():
        await_block(tp - 2)

    def last_step(m, _):
        part[...] = share(late_tile(m), place)
        for role, copy, buf, _physical in flows:
            @pl.when(role == 1)
            def _():
                part[...] += dot(buf[1, 0, m], extra[column_block(tp - 2, place == 1)])

            @pl.when(role >= 2)
            def _():
                copy(buf.at[1, inner - 1, m], 1, inner - 1, m).wait_recv()
                part[...] += buf[1, inner - 1, m].astype(F32)

        out_ref[late_tile(m), :] = part[...].astype(BF16)
        part[...] = share(early_tile(m), place)
        for role, copy, buf, _physical in flows:
            @pl.when(role == 1)
            def _():
                copy(buf.at[1, 1, m], 1, 1, m).wait_recv()
                part[...] += buf[1, 1, m].astype(F32)

            @pl.when(role >= 2)
            def _():
                copy(buf.at[0, inner - 1, m], 0, inner - 1, m).wait_recv()
                part[...] += buf[0, inner - 1, m].astype(F32)

        out_ref[early_tile(m), :] = part[...].astype(BF16)
        return 0

    lax.fori_loop(0, tiles, last_step, 0)

    def sent_step(t, _):
        i = t // tiles
        m = t % tiles
        for role, copy, buf, _physical in flows:
            for h in range(2):
                early_end = (role == 0) if h == 0 else (role == 0) & (i < 2)

                @pl.when(early_end | ((role > 0) & (i >= role - 1)))
                def _():
                    copy(buf.at[h, i, m], h, i, m).wait_send()
        return 0

    lax.fori_loop(0, steps, sent_step, 0)
    lax.fori_loop(1, ctx - me, lambda d, _: (to_peer(d).wait_send(), 0)[1], 0)

    @pl.when((place == 0) | (far == 0))
    def _():
        lax.fori_loop(0, tp - 1, lambda o, _: (hop(o, place == 0).wait_send(), 0)[1], 0)

    @pl.when(is_helper)
    def _():
        for order in range(tp - 1):
            lax.fori_loop(1, chips, lambda d, _: (across(order, d).wait_send(), 0)[1], 0)
            lax.fori_loop(0, chips, lambda d, _: (beside(order, d).wait_send(), 0)[1], 0)


def on_device(ctx, tp, query, keys, values, residues, rates, w_out):
    block, width = keys.shape
    state = rates.shape[1]
    chunk = math.gcd(block, LANES)
    chunks = block // chunk
    half = chunks // 2
    groups = LANES // SHARE
    modes = groups * state
    lane_blocks = width // LANES
    tiles = 4
    inner = tp - 2
    rows = block // (2 * tiles)
    at_row = np.arange(modes) // state
    gmask = jnp.asarray((at_row[:, None] == np.arange(LANES)[None, :] // SHARE).astype(np.float32))
    smask = jnp.asarray((np.arange(groups)[:, None] == at_row[None, :]).astype(np.float32))
    vmem = pl.BlockSpec(memory_space=pltpu.VMEM)
    hbm = pl.BlockSpec(memory_space=pl.ANY)
    dma = pltpu.SemaphoreType.DMA
    return pl.pallas_call(
        functools.partial(layer_kernel, ctx, tp, tiles, state, chunk),
        out_shape=jax.ShapeDtypeStruct((block, width), BF16),
        in_specs=[hbm] * 4 + [vmem] * 4,
        out_specs=vmem,
        scratch_shapes=[
            pltpu.VMEM((block, width), BF16),
            pltpu.VMEM((block, width), BF16),
            pltpu.VMEM((block, width), BF16),
            pltpu.VMEM(w_out.shape, BF16),
            pltpu.VMEM((lane_blocks, modes, LANES), F32),
            pltpu.VMEM((lane_blocks, 8, modes), F32),
            pltpu.VMEM((lane_blocks, 8, modes), F32),
            pltpu.VMEM((block, width), BF16),
            pltpu.VMEM((ctx, state, width), F32),
            pltpu.VMEM((state, width), F32),
            pltpu.VMEM((chunks, state, width), F32),
            pltpu.VMEM((lane_blocks, chunk, half * LANES), F32),
            pltpu.VMEM((groups * chunk, half * LANES), BF16),
            pltpu.VMEM((lane_blocks, chunk, groups * chunk), BF16),
            pltpu.VMEM((3 * modes, half * LANES), BF16),
            pltpu.VMEM((tp - 1, width, width), BF16),
            pltpu.VMEM((2, inner, tiles, rows, width), BF16),
            pltpu.VMEM((2, inner, tiles, rows, width), BF16),
            pltpu.VMEM((inner, tiles, rows, width), BF16),
            pltpu.VMEM((rows, width), F32),
            dma((4,)),
            dma((ctx,)),
            dma((ctx,)),
            dma((tp - 1,)),
            dma((tp - 1,)),
            dma((tp - 1, ctx)),
            dma((tp - 1, ctx)),
            dma((2, inner, tiles)),
            dma((2, inner, tiles)),
            dma((2, inner, tiles)),
            dma((2, inner, tiles)),
        ],
        compiler_params=pltpu.CompilerParams(
            collective_id=0, has_side_effects=True, vmem_limit_bytes=50 * 2**20),
        cost_estimate=pl.CostEstimate(
            flops=4 * block * width * width * tp, bytes_accessed=24 * block * width, transcendentals=0),
        name="hyena_layer",
    )(query, keys, values, w_out, rates.T, residues.T, gmask, smask)


def solution(mesh):
    in_specs = (P("ctx", "tp"), P("ctx", "tp"), P("ctx", "tp"), P(), P(), P("tp", None))
    return jax.shard_map(
        functools.partial(on_device, mesh.shape["ctx"], mesh.shape["tp"]),
        mesh=mesh, in_specs=in_specs, out_specs=P("ctx", "tp"), check_vma=False)
```

```python
import functools
import math

import jax
import jax.numpy as jnp
from jax import lax
from jax.experimental import pallas as pl
from jax.experimental.pallas import tpu as pltpu
from jax.sharding import PartitionSpec as P

SHARE = 16
LANES = 128
SUBS = 4
MESH = pl.DeviceIdType.MESH
F32 = jnp.float32
BF16 = jnp.bfloat16


def split(x):
    upper = x.astype(BF16)
    return upper, (x - upper.astype(F32)).astype(BF16)


def dot(a, b):
    return jnp.dot(a, b, preferred_element_type=F32)


def layer_kernel(ctx, tp, tiles, state, chunk, q_hbm, k_hbm, v_hbm, w_hbm, rates_hbm, residues_hbm,
                 out_ref, rates_ref, residues_ref, gmask_ref, smask_ref, q_ref, k_ref, v_ref, w_ref, columns, rate_rows, gain_rows, gated, states, own, before,
                 inside, wide, taps, carry, extra, right_buf, left_buf, stage, part, early_part, load_sem, state_send, state_recv, hop_send,
                 hop_recv, spread_send, spread_recv, right_send, right_recv, left_send, left_recv):
    block, width = out_ref.shape
    chunks = block // chunk
    span = chunks // 4
    lane_blocks = width // LANES
    groups = LANES // SHARE
    modes = groups * state
    rows = block // (2 * tiles)
    subs = SUBS
    some = rows // subs
    piece = width // ctx
    inner = tp - 2
    me = lax.axis_index("ctx")
    place = lax.axis_index("tp")
    far = tp - 1 - place
    has_left = place > 0
    has_right = far > 0
    is_helper = (place == 1) | (far == 1)

    loads = [pltpu.make_async_copy(src, dst, load_sem.at[i]) for i, (src, dst) in enumerate(
        [(k_hbm, k_ref), (v_hbm, v_ref), (q_hbm, q_ref), (w_hbm, w_ref), (rates_hbm, rates_ref),
         (residues_hbm, residues_ref)])]
    for at in (4, 5, 0, 1):
        loads[at].start()

    barrier = pltpu.get_barrier_semaphore()

    def greet(d, _):
        pl.semaphore_signal(barrier, inc=1, device_id={"ctx": lax.rem(me + d, ctx)}, device_id_type=MESH)
        return 0

    lax.fori_loop(1, ctx, greet, 0)

    @pl.when(has_left)
    def _():
        pl.semaphore_signal(barrier, inc=1, device_id={"tp": place - 1}, device_id_type=MESH)

    @pl.when(has_right)
    def _():
        pl.semaphore_signal(barrier, inc=1, device_id={"tp": place + 1}, device_id_type=MESH)

    pl.semaphore_wait(barrier, ctx - 1 + has_left.astype(jnp.int32) + has_right.astype(jnp.int32))

    def column_block(order, from_left):
        return jnp.where(from_left, tp - 2 - order, order)

    def piece_rows(j):
        return pl.ds(pl.multiple_of(j * piece, piece), piece)

    def hop(order, to_right):
        e = column_block(order, to_right)
        cols = pl.ds(pl.multiple_of(jnp.where(to_right, e + 1, e) * width, width), width)
        return pltpu.make_async_remote_copy(
            src_ref=w_hbm.at[piece_rows(me), cols], dst_ref=extra.at[e, piece_rows(me)],
            send_sem=hop_send.at[e], recv_sem=hop_recv.at[e],
            device_id={"tp": jnp.where(to_right, place + 1, place - 1)}, device_id_type=MESH)

    def hop_step(order, _):
        hop(order, place == 0).start()
        return 0

    @pl.when((place == 0) | (far == 0))
    def _():
        lax.fori_loop(0, tp - 1, hop_step, 0)

    chips = ctx // 2
    sibling = me + 1 - 2 * lax.rem(me, 2)

    def chip_peer(d):
        return lax.rem(me + 2 * d, ctx)

    def carried(order, j, send, peer):
        e = column_block(order, place == 1)
        return pltpu.make_async_remote_copy(
            src_ref=extra.at[e, piece_rows(j)], dst_ref=extra.at[e, piece_rows(j)],
            send_sem=spread_send.at[e, send], recv_sem=spread_recv.at[e, j],
            device_id={"ctx": peer}, device_id_type=MESH)

    def across(order, d):
        return carried(order, me, d, chip_peer(d))

    def beside(order, d):
        return carried(order, chip_peer(d), chips + d, sibling)

    def spread_block(order):
        e = column_block(order, place == 1)
        pltpu.make_async_remote_copy(
            src_ref=w_hbm.at[piece_rows(me), pl.ds(0, width)], dst_ref=extra.at[e, piece_rows(me)],
            send_sem=hop_send.at[e], recv_sem=hop_recv.at[e],
            device_id={"tp": jnp.where(place == 1, place - 1, place + 1)}, device_id_type=MESH).wait_recv()
        lax.fori_loop(1, chips, lambda d, _: (across(order, d).start(), 0)[1], 0)
        beside(order, 0).start()

    def relay_block(order):
        def relay(d, _):
            carried(order, chip_peer(d), d, chip_peer(d)).wait_recv()
            beside(order, d).start()
            return 0

        lax.fori_loop(1, chips, relay, 0)

    def await_block(order):
        def arrived(d, _):
            j = lax.rem(sibling + 2 * d, ctx)
            carried(order, j, chips + d, sibling).wait_recv()
            return 0

        lax.fori_loop(0, chips, arrived, 0)

    def product(k, lanes):
        at = pl.ds(pl.multiple_of(k * chunk, chunk), chunk)
        return (k_ref[at, lanes].astype(F32) * v_ref[at, lanes].astype(F32)).astype(BF16)

    def lanes_of(b):
        return pl.ds(pl.multiple_of(b * LANES, LANES), LANES)

    def spread_rows(ref, b):
        every = ref.shape[1]
        tall = jnp.concatenate([ref[...]] * groups, axis=0)
        lane = lax.broadcasted_iota(jnp.int32, (groups, state, every), 2)
        group = lax.broadcasted_iota(jnp.int32, (groups, state, every), 0)
        first = (place * lane_blocks + b) * groups
        chosen = jnp.where(lane == group + first, tall.reshape(groups, state, every), 0.0)
        column = chosen.sum(axis=2, keepdims=True).reshape(modes, 1)
        return jnp.broadcast_to(column, (modes, LANES))

    def table_step(b, _):
        rate = spread_rows(rates_ref, b)
        columns[b] = rate
        rate_rows[b] = rate.T[0:8, :]
        gain_rows[b] = (spread_rows(residues_ref, b) * jnp.sqrt(2.0 * rate)).T[0:8, :]
        return 0

    def rate_row(b):
        return rate_rows[b, 0:1, :]

    def gain_row(b):
        return gain_rows[b, 0:1, :]

    def rate_columns(b):
        return columns[b]

    def rate_lanes(b):
        return (rate_columns(b) * gmask_ref[...]).reshape(groups, state, LANES).sum(0)

    def state_step(b, _):
        lanes = lanes_of(b)
        tau = lax.broadcasted_iota(jnp.int32, (modes, chunk), 1).astype(F32)
        fading = jnp.concatenate(split(jnp.exp(-rate_columns(b) * (chunk - 1.0 - tau))), axis=0)
        decay = jnp.exp(-rate_lanes(b) * float(chunk))
        gmask = gmask_ref[...]
        fresh = dot(fading, jnp.concatenate([product(k, lanes) for k in range(chunks)], axis=1))
        fresh = fresh[:modes] + fresh[modes:]
        total = jnp.zeros((state, LANES), F32)
        for k in range(chunks):
            before[k, :, lanes] = total
            new = fresh[:, k * LANES:(k + 1) * LANES] * gmask
            total = total * decay + new.reshape(groups, state, LANES).sum(0)
        own[:, lanes] = total
        return 0


    def to_peer(d):
        return pltpu.make_async_remote_copy(
            src_ref=own, dst_ref=states.at[me], send_sem=state_send.at[d], recv_sem=state_recv.at[me],
            device_id={"ctx": lax.rem(me + d, ctx)}, device_id_type=MESH)

    def from_peer(j):
        return pltpu.make_async_remote_copy(
            src_ref=own, dst_ref=states.at[j], send_sem=state_send.at[0], recv_sem=state_recv.at[j],
            device_id={"ctx": j}, device_id_type=MESH)

    def taps_step(b, _):
        row = lax.broadcasted_iota(jnp.int32, (chunk, modes), 0).astype(F32)
        col = lax.broadcasted_iota(jnp.int32, (modes, chunk), 1).astype(F32)
        middle = chunk / 2.0
        falling = gain_row(b) * jnp.exp(-rate_row(b) * (row - middle))
        b_hi, b_lo = split(jnp.exp(rate_columns(b) * (col - middle)))
        causal = lax.broadcasted_iota(jnp.int32, (chunk, chunk), 0) >= lax.broadcasted_iota(
            jnp.int32, (chunk, chunk), 1)
        a_hi, a_lo = split(jnp.concatenate([falling * smask_ref[g:g + 1, :] for g in range(groups)], axis=0))
        tap = dot(jnp.concatenate([a_hi, a_lo, a_hi], axis=1), jnp.concatenate([b_hi, b_hi, b_lo], axis=0))
        for g in range(groups):
            own_tap = jnp.where(causal, tap[g * chunk:(g + 1) * chunk], 0.0)
            taps[b, :, g * chunk:(g + 1) * chunk] = own_tap.astype(BF16)
        return 0

    def inside_step(b, first):
        lanes = lanes_of(b)
        xs = [product(first + k, lanes) for k in range(span)]
        for g in range(groups):
            only = gmask_ref[g * state:g * state + 1, :].astype(BF16)
            for k in range(span):
                wide[g * chunk:(g + 1) * chunk, k * LANES:(k + 1) * LANES] = xs[k] * only
        inside[b] = dot(taps[b], wide[...])

    def carry_step(b, first):
        lanes = lanes_of(b)
        rlane = rate_lanes(b)
        along = jnp.exp(-rlane * float(block))
        decay = jnp.exp(-rlane * float(chunk))
        reached = lax.fori_loop(
            0, me, lambda j, r: r * along + states[j, :, lanes], jnp.zeros((state, LANES), F32))
        reached = reached * jnp.exp(-rlane * (chunk * first).astype(F32))
        gmask = gmask_ref[...]
        for k in range(span):
            entering = before[first + k, :, lanes] + reached
            reached = reached * decay
            hi, lo = split(jnp.concatenate([entering] * groups, axis=0) * gmask)
            at = slice(k * LANES, (k + 1) * LANES)
            carry[0:modes, at] = hi
            carry[modes:2 * modes, at] = hi
            carry[2 * modes:3 * modes, at] = lo
        row = lax.broadcasted_iota(jnp.int32, (chunk, modes), 0).astype(F32)
        hi, lo = split(gain_row(b) * jnp.exp(-rate_row(b) * (row + 1.0)))
        full = inside[b] + dot(jnp.concatenate([hi, lo, hi], axis=1), carry[...])
        for k in range(span):
            at = pl.ds(pl.multiple_of((first + k) * chunk, chunk), chunk)
            convolved = full[:, k * LANES:(k + 1) * LANES].astype(BF16)
            gated[at, lanes] = (q_ref[at, lanes].astype(F32) * convolved.astype(F32)).astype(BF16)

    def early_inside(b, _):
        inside_step(b, 0)
        return 0

    def early_carry(b, _):
        carry_step(b, jnp.int32(0))
        return 0

    rest = 3 * lane_blocks
    batch = max(1, lane_blocks // 2)

    def late_step(item, _):
        b = item % lane_blocks
        first = (1 + item // lane_blocks) * span
        inside_step(b, first)
        carry_step(b, first)
        return 0

    group = lax.broadcasted_iota(jnp.int32, (groups, state, LANES), 0) * SHARE
    lane = lax.broadcasted_iota(jnp.int32, (groups, state, LANES), 2)
    gmask_ref[...] = jnp.where((lane >= group) & (lane < group + SHARE), 1.0, 0.0).reshape(modes, LANES)
    group = lax.broadcasted_iota(jnp.int32, (groups, modes), 0) * state
    lane = lax.broadcasted_iota(jnp.int32, (groups, modes), 1)
    smask_ref[...] = jnp.where((lane >= group) & (lane < group + state), 1.0, 0.0)
    loads[4].wait()
    loads[5].wait()
    lax.fori_loop(0, lane_blocks, table_step, 0)
    loads[0].wait()
    loads[1].wait()
    loads[2].start()
    loads[3].start()
    lax.fori_loop(0, lane_blocks, state_step, 0)
    lax.fori_loop(1, ctx - me, lambda d, _: (to_peer(d).start(), 0)[1], 0)
    lax.fori_loop(0, lane_blocks, taps_step, 0)
    lax.fori_loop(0, lane_blocks, early_inside, 0)
    lax.fori_loop(0, me, lambda j, _: (from_peer(j).wait_recv(), 0)[1], 0)
    loads[2].wait()
    lax.fori_loop(0, lane_blocks, early_carry, 0)
    loads[3].wait()

    def early_tile(m):
        return pl.ds(pl.multiple_of(m * rows, rows), rows)

    def late_tile(m):
        return pl.ds(pl.multiple_of((tiles + m) * rows, rows), rows)

    def share(tile, dest):
        cols = pl.ds(pl.multiple_of(dest * width, width), width)
        return dot(gated[tile, :], w_ref[:, cols])

    def some_rows(u):
        return pl.ds(pl.multiple_of(u * some, some), some)

    def rightward(src, h, i, m, u):
        return pltpu.make_async_remote_copy(
            src_ref=src, dst_ref=right_buf.at[h, i, m, some_rows(u)], send_sem=right_send.at[h, i, m, u],
            recv_sem=right_recv.at[h, i, m, u], device_id={"tp": place + 1}, device_id_type=MESH)

    def leftward(src, h, i, m, u):
        return pltpu.make_async_remote_copy(
            src_ref=src, dst_ref=left_buf.at[h, i, m, some_rows(u)], send_sem=left_send.at[h, i, m, u],
            recv_sem=left_recv.at[h, i, m, u], device_id={"tp": place - 1}, device_id_type=MESH)

    def each(body):
        lax.fori_loop(0, subs, lambda u, _: (body(u), 0)[1], 0)

    def received(copy, buf, h, i, m, u):
        copy(buf.at[h, i, m, some_rows(u)], h, i, m, u).wait_recv()

    flows = ((place, rightward, right_buf, lambda d: d), (far, leftward, left_buf, lambda d: tp - 1 - d))

    def sums_step(flow, h, i, m, tile, go):
        role, copy, buf, physical = flow
        came = i - (role >= 2).astype(jnp.int32)
        dest = tp - 1 - i + jnp.maximum(role - 1, 0)

        @pl.when(go)
        def _():
            part[...] = share(tile, physical(dest))

        @pl.when(go & (role > 0))
        def _():
            def add(u):
                at = some_rows(u)
                received(copy, buf, h, came, m, u)
                buf[h, came, m, at] = (part[at, :] + buf[h, came, m, at].astype(F32)).astype(BF16)
                copy(buf.at[h, came, m, at], h, i, m, u).start()

            each(add)

        @pl.when(go & (role == 0))
        def _():
            buf[h, came, m] = part[...].astype(BF16)
            each(lambda u: copy(buf.at[h, came, m, some_rows(u)], h, i, m, u).start())

    steps = inner * tiles

    def early_step(t, _):
        i = t // tiles
        m = t % tiles
        for flow in flows:
            sums_step(flow, 0, i, m, early_tile(m), i >= flow[0] - 1)

        @pl.when(is_helper & (t < tp - 1))
        def _():
            spread_block(t)

        @pl.when(is_helper & (t >= steps - (tp - 1)))
        def _():
            relay_block(t - (steps - (tp - 1)))

        lax.fori_loop(jnp.minimum(t * batch, rest), jnp.minimum(t * batch + batch, rest), late_step, 0)
        return 0

    lax.fori_loop(0, steps, early_step, 0)
    lax.fori_loop(min(steps * batch, rest), rest, late_step, 0)

    def end_step(flow, i, m):
        role, copy, buf, physical = flow

        @pl.when((role == 0) & (i == 0))
        def _():
            def send(u):
                at = pl.ds(pl.multiple_of((tiles + m) * rows + u * some, some), some)
                copy(gated.at[at], 1, 0, m, u).start()

            each(send)

        @pl.when((role == 0) & (i == 1))
        def _():
            buf[1, 1, m] = share(early_tile(m), physical(1)).astype(BF16)
            each(lambda u: copy(buf.at[1, 1, m, some_rows(u)], 1, 1, m, u).start())

    def helper_step(flow, i, m):
        role, copy, buf, physical = flow

        @pl.when(role == 1)
        def _():
            part[...] = share(late_tile(m), physical(tp - 1 - i))

            @pl.when(i == 0)
            def _():
                each(lambda u: received(copy, buf, 1, 0, m, u))

            @pl.when(m == 0)
            def _():
                await_block(i)

            stage[i, m] = (part[...] + dot(buf[1, 0, m], extra[column_block(i, place == 1)])).astype(BF16)
            each(lambda u: copy(stage.at[i, m, some_rows(u)], 1, i, m, u).start())

    def late_sums(t, _):
        i = t // tiles
        m = t % tiles
        for flow in flows:
            end_step(flow, i, m)
            helper_step(flow, i, m)
            sums_step(flow, 1, i, m, late_tile(m), (flow[0] >= 2) & (i >= flow[0] - 1))
        return 0

    lax.fori_loop(0, steps, late_sums, 0)

    @pl.when(is_helper)
    def _():
        await_block(tp - 2)

    def last_step(m, _):
        part[...] = share(late_tile(m), place)
        early_part[...] = share(early_tile(m), place)
        for role, copy, buf, _physical in flows:
            @pl.when(role == 1)
            def _():
                part[...] += dot(buf[1, 0, m], extra[column_block(tp - 2, place == 1)])

        for role, copy, buf, _physical in flows:
            @pl.when(role == 1)
            def _():
                each(lambda u: received(copy, buf, 1, 1, m, u))
                early_part[...] += buf[1, 1, m].astype(F32)

            @pl.when(role >= 2)
            def _():
                each(lambda u: received(copy, buf, 0, inner - 1, m, u))
                early_part[...] += buf[0, inner - 1, m].astype(F32)
                each(lambda u: received(copy, buf, 1, inner - 1, m, u))
                part[...] += buf[1, inner - 1, m].astype(F32)

        out_ref[late_tile(m), :] = part[...].astype(BF16)
        out_ref[early_tile(m), :] = early_part[...].astype(BF16)
        return 0

    lax.fori_loop(0, tiles, last_step, 0)

    def sent_step(t, _):
        i = t // tiles
        m = t % tiles
        for role, copy, buf, _physical in flows:
            for h in range(2):
                early_end = (role == 0) if h == 0 else (role == 0) & (i < 2)

                @pl.when(early_end | ((role > 0) & (i >= role - 1)))
                def _():
                    each(lambda u: copy(buf.at[h, i, m, some_rows(u)], h, i, m, u).wait_send())
        return 0

    lax.fori_loop(0, steps, sent_step, 0)
    lax.fori_loop(1, ctx - me, lambda d, _: (to_peer(d).wait_send(), 0)[1], 0)

    @pl.when((place == 0) | (far == 0))
    def _():
        lax.fori_loop(0, tp - 1, lambda o, _: (hop(o, place == 0).wait_send(), 0)[1], 0)

    @pl.when(is_helper)
    def _():
        for order in range(tp - 1):
            lax.fori_loop(1, chips, lambda d, _: (across(order, d).wait_send(), 0)[1], 0)
            lax.fori_loop(0, chips, lambda d, _: (beside(order, d).wait_send(), 0)[1], 0)


def on_device(ctx, tp, query, keys, values, residues, rates, w_out):
    block, width = keys.shape
    state = rates.shape[1]
    chunk = math.gcd(block, LANES)
    chunks = block // chunk
    span = chunks // 4
    groups = LANES // SHARE
    modes = groups * state
    lane_blocks = width // LANES
    tiles = 4
    inner = tp - 2
    rows = block // (2 * tiles)
    vmem = pl.BlockSpec(memory_space=pltpu.VMEM)
    hbm = pl.BlockSpec(memory_space=pltpu.HBM)
    dma = pltpu.SemaphoreType.DMA
    return pl.pallas_call(
        functools.partial(layer_kernel, ctx, tp, tiles, state, chunk),
        out_shape=jax.ShapeDtypeStruct((block, width), BF16),
        in_specs=[hbm] * 6,
        out_specs=vmem,
        scratch_shapes=[
            pltpu.VMEM((state, rates.shape[0]), F32),
            pltpu.VMEM((state, rates.shape[0]), F32),
            pltpu.VMEM((modes, LANES), F32),
            pltpu.VMEM((groups, modes), F32),
            pltpu.VMEM((block, width), BF16),
            pltpu.VMEM((block, width), BF16),
            pltpu.VMEM((block, width), BF16),
            pltpu.VMEM(w_out.shape, BF16),
            pltpu.VMEM((lane_blocks, modes, LANES), F32),
            pltpu.VMEM((lane_blocks, 8, modes), F32),
            pltpu.VMEM((lane_blocks, 8, modes), F32),
            pltpu.VMEM((block, width), BF16),
            pltpu.VMEM((ctx, state, width), F32),
            pltpu.VMEM((state, width), F32),
            pltpu.VMEM((chunks, state, width), F32),
            pltpu.VMEM((lane_blocks, chunk, span * LANES), F32),
            pltpu.VMEM((groups * chunk, span * LANES), BF16),
            pltpu.VMEM((lane_blocks, chunk, groups * chunk), BF16),
            pltpu.VMEM((3 * modes, span * LANES), BF16),
            pltpu.VMEM((tp - 1, width, width), BF16),
            pltpu.VMEM((2, inner, tiles, rows, width), BF16),
            pltpu.VMEM((2, inner, tiles, rows, width), BF16),
            pltpu.VMEM((inner, tiles, rows, width), BF16),
            pltpu.VMEM((rows, width), F32),
            pltpu.VMEM((rows, width), F32),
            dma((6,)),
            dma((ctx,)),
            dma((ctx,)),
            dma((tp - 1,)),
            dma((tp - 1,)),
            dma((tp - 1, ctx)),
            dma((tp - 1, ctx)),
            dma((2, inner, tiles, SUBS)),
            dma((2, inner, tiles, SUBS)),
            dma((2, inner, tiles, SUBS)),
            dma((2, inner, tiles, SUBS)),
        ],
        compiler_params=pltpu.CompilerParams(
            collective_id=0, has_side_effects=True, vmem_limit_bytes=50 * 2**20),
        cost_estimate=pl.CostEstimate(
            flops=4 * block * width * width * tp, bytes_accessed=24 * block * width, transcendentals=0),
        name="hyena_layer",
    )(query, keys, values, w_out, rates.T, residues.T)


def solution(mesh):
    in_specs = (P("ctx", "tp"), P("ctx", "tp"), P("ctx", "tp"), P(), P(), P("tp", None))
    return jax.shard_map(
        functools.partial(on_device, mesh.shape["ctx"], mesh.shape["tp"]),
        mesh=mesh, in_specs=in_specs, out_specs=P("ctx", "tp"), check_vma=False)
```

```python
import functools
import math

import jax
import jax.numpy as jnp
from jax import lax
from jax.experimental import pallas as pl
from jax.experimental.pallas import tpu as pltpu
from jax.sharding import PartitionSpec as P

SHARE = 16
LANES = 128
SUBS = 4
MESH = pl.DeviceIdType.MESH
F32 = jnp.float32
BF16 = jnp.bfloat16


def split(x):
    upper = x.astype(BF16)
    return upper, (x - upper.astype(F32)).astype(BF16)


def dot(a, b):
    return jnp.dot(a, b, preferred_element_type=F32)


def layer_kernel(ctx, tp, early, late, state, chunk, q_hbm, k_hbm, v_hbm, w_hbm, rates_hbm, residues_hbm,
                 out_ref, rates_ref, residues_ref, gmask_ref, smask_ref, q_ref, k_ref, v_ref, w_ref, columns, rate_rows, gain_rows, gated, states, own, before,
                 inside, wide, taps, carry, extra, right_buf, left_buf, stage, part, load_sem, state_send, state_recv, hop_send,
                 hop_recv, spread_send, spread_recv, right_send, right_recv, left_send, left_recv):
    block, width = out_ref.shape
    chunks = block // chunk
    span = chunks // 4
    lane_blocks = width // LANES
    groups = LANES // SHARE
    modes = groups * state
    rows = block // (early + late)
    subs = SUBS
    some = rows // subs
    piece = width // ctx
    inner = tp - 2
    me = lax.axis_index("ctx")
    place = lax.axis_index("tp")
    far = tp - 1 - place
    has_left = place > 0
    has_right = far > 0
    is_helper = (place == 1) | (far == 1)

    loads = [pltpu.make_async_copy(src, dst, load_sem.at[i]) for i, (src, dst) in enumerate(
        [(k_hbm, k_ref), (v_hbm, v_ref), (q_hbm, q_ref), (w_hbm, w_ref), (rates_hbm, rates_ref),
         (residues_hbm, residues_ref)])]
    for at in (4, 5, 0, 1):
        loads[at].start()

    barrier = pltpu.get_barrier_semaphore()

    def greet(d, _):
        pl.semaphore_signal(barrier, inc=1, device_id={"ctx": lax.rem(me + d, ctx)}, device_id_type=MESH)
        return 0

    lax.fori_loop(1, ctx, greet, 0)

    @pl.when(has_left)
    def _():
        pl.semaphore_signal(barrier, inc=1, device_id={"tp": place - 1}, device_id_type=MESH)

    @pl.when(has_right)
    def _():
        pl.semaphore_signal(barrier, inc=1, device_id={"tp": place + 1}, device_id_type=MESH)

    pl.semaphore_wait(barrier, ctx - 1 + has_left.astype(jnp.int32) + has_right.astype(jnp.int32))

    def column_block(order, from_left):
        return jnp.where(from_left, tp - 2 - order, order)

    def piece_rows(j):
        return pl.ds(pl.multiple_of(j * piece, piece), piece)

    def hop(order, to_right):
        e = column_block(order, to_right)
        cols = pl.ds(pl.multiple_of(jnp.where(to_right, e + 1, e) * width, width), width)
        return pltpu.make_async_remote_copy(
            src_ref=w_hbm.at[piece_rows(me), cols], dst_ref=extra.at[e, piece_rows(me)],
            send_sem=hop_send.at[e], recv_sem=hop_recv.at[e],
            device_id={"tp": jnp.where(to_right, place + 1, place - 1)}, device_id_type=MESH)

    def hop_step(order, _):
        hop(order, place == 0).start()
        return 0

    @pl.when((place == 0) | (far == 0))
    def _():
        lax.fori_loop(0, inner, hop_step, 0)

    chips = ctx // 2
    sibling = me + 1 - 2 * lax.rem(me, 2)

    def chip_peer(d):
        return lax.rem(me + 2 * d, ctx)

    def carried(order, j, send, peer):
        e = column_block(order, place == 1)
        return pltpu.make_async_remote_copy(
            src_ref=extra.at[e, piece_rows(j)], dst_ref=extra.at[e, piece_rows(j)],
            send_sem=spread_send.at[e, send], recv_sem=spread_recv.at[e, j],
            device_id={"ctx": peer}, device_id_type=MESH)

    def across(order, d):
        return carried(order, me, d, chip_peer(d))

    def beside(order, d):
        return carried(order, chip_peer(d), chips + d, sibling)

    def spread_block(order):
        e = column_block(order, place == 1)
        pltpu.make_async_remote_copy(
            src_ref=w_hbm.at[piece_rows(me), pl.ds(0, width)], dst_ref=extra.at[e, piece_rows(me)],
            send_sem=hop_send.at[e], recv_sem=hop_recv.at[e],
            device_id={"tp": jnp.where(place == 1, place - 1, place + 1)}, device_id_type=MESH).wait_recv()
        lax.fori_loop(1, chips, lambda d, _: (across(order, d).start(), 0)[1], 0)
        beside(order, 0).start()

    def relay_block(order):
        def relay(d, _):
            carried(order, chip_peer(d), d, chip_peer(d)).wait_recv()
            beside(order, d).start()
            return 0

        lax.fori_loop(1, chips, relay, 0)

    def await_block(order):
        def arrived(d, _):
            j = lax.rem(sibling + 2 * d, ctx)
            carried(order, j, chips + d, sibling).wait_recv()
            return 0

        lax.fori_loop(0, chips, arrived, 0)

    def product(k, lanes):
        at = pl.ds(pl.multiple_of(k * chunk, chunk), chunk)
        return (k_ref[at, lanes].astype(F32) * v_ref[at, lanes].astype(F32)).astype(BF16)

    def lanes_of(b):
        return pl.ds(pl.multiple_of(b * LANES, LANES), LANES)

    def spread_rows(ref, b):
        every = ref.shape[1]
        tall = jnp.concatenate([ref[...]] * groups, axis=0)
        lane = lax.broadcasted_iota(jnp.int32, (groups, state, every), 2)
        group = lax.broadcasted_iota(jnp.int32, (groups, state, every), 0)
        first = (place * lane_blocks + b) * groups
        chosen = jnp.where(lane == group + first, tall.reshape(groups, state, every), 0.0)
        column = chosen.sum(axis=2, keepdims=True).reshape(modes, 1)
        return jnp.broadcast_to(column, (modes, LANES))

    def table_step(b, _):
        rate = spread_rows(rates_ref, b)
        columns[b] = rate
        rate_rows[b] = rate.T[0:8, :]
        gain_rows[b] = (spread_rows(residues_ref, b) * jnp.sqrt(2.0 * rate)).T[0:8, :]
        return 0

    def rate_row(b):
        return rate_rows[b, 0:1, :]

    def gain_row(b):
        return gain_rows[b, 0:1, :]

    def rate_columns(b):
        return columns[b]

    def rate_lanes(b):
        return (rate_columns(b) * gmask_ref[...]).reshape(groups, state, LANES).sum(0)

    def state_step(b, _):
        lanes = lanes_of(b)
        tau = lax.broadcasted_iota(jnp.int32, (modes, chunk), 1).astype(F32)
        fading = jnp.concatenate(split(jnp.exp(-rate_columns(b) * (chunk - 1.0 - tau))), axis=0)
        decay = jnp.exp(-rate_lanes(b) * float(chunk))
        gmask = gmask_ref[...]
        fresh = dot(fading, jnp.concatenate([product(k, lanes) for k in range(chunks)], axis=1))
        fresh = fresh[:modes] + fresh[modes:]
        total = jnp.zeros((state, LANES), F32)
        for k in range(chunks):
            before[k, :, lanes] = total
            new = fresh[:, k * LANES:(k + 1) * LANES] * gmask
            total = total * decay + new.reshape(groups, state, LANES).sum(0)
        own[:, lanes] = total
        return 0


    def to_peer(d):
        return pltpu.make_async_remote_copy(
            src_ref=own, dst_ref=states.at[me], send_sem=state_send.at[d], recv_sem=state_recv.at[me],
            device_id={"ctx": lax.rem(me + d, ctx)}, device_id_type=MESH)

    def from_peer(j):
        return pltpu.make_async_remote_copy(
            src_ref=own, dst_ref=states.at[j], send_sem=state_send.at[0], recv_sem=state_recv.at[j],
            device_id={"ctx": j}, device_id_type=MESH)

    def taps_step(b, _):
        row = lax.broadcasted_iota(jnp.int32, (chunk, modes), 0).astype(F32)
        col = lax.broadcasted_iota(jnp.int32, (modes, chunk), 1).astype(F32)
        middle = chunk / 2.0
        falling = gain_row(b) * jnp.exp(-rate_row(b) * (row - middle))
        b_hi, b_lo = split(jnp.exp(rate_columns(b) * (col - middle)))
        causal = lax.broadcasted_iota(jnp.int32, (chunk, chunk), 0) >= lax.broadcasted_iota(
            jnp.int32, (chunk, chunk), 1)
        a_hi, a_lo = split(jnp.concatenate([falling * smask_ref[g:g + 1, :] for g in range(groups)], axis=0))
        tap = dot(jnp.concatenate([a_hi, a_lo, a_hi], axis=1), jnp.concatenate([b_hi, b_hi, b_lo], axis=0))
        for g in range(groups):
            own_tap = jnp.where(causal, tap[g * chunk:(g + 1) * chunk], 0.0)
            taps[b, :, g * chunk:(g + 1) * chunk] = own_tap.astype(BF16)
        return 0

    def inside_step(b, first):
        lanes = lanes_of(b)
        xs = [product(first + k, lanes) for k in range(span)]
        for g in range(groups):
            only = gmask_ref[g * state:g * state + 1, :].astype(BF16)
            for k in range(span):
                wide[g * chunk:(g + 1) * chunk, k * LANES:(k + 1) * LANES] = xs[k] * only
        inside[b] = dot(taps[b], wide[...])

    def carry_step(b, first):
        lanes = lanes_of(b)
        rlane = rate_lanes(b)
        along = jnp.exp(-rlane * float(block))
        decay = jnp.exp(-rlane * float(chunk))
        reached = lax.fori_loop(
            0, me, lambda j, r: r * along + states[j, :, lanes], jnp.zeros((state, LANES), F32))
        reached = reached * jnp.exp(-rlane * (chunk * first).astype(F32))
        gmask = gmask_ref[...]
        for k in range(span):
            entering = before[first + k, :, lanes] + reached
            reached = reached * decay
            hi, lo = split(jnp.concatenate([entering] * groups, axis=0) * gmask)
            at = slice(k * LANES, (k + 1) * LANES)
            carry[0:modes, at] = hi
            carry[modes:2 * modes, at] = hi
            carry[2 * modes:3 * modes, at] = lo
        row = lax.broadcasted_iota(jnp.int32, (chunk, modes), 0).astype(F32)
        hi, lo = split(gain_row(b) * jnp.exp(-rate_row(b) * (row + 1.0)))
        full = inside[b] + dot(jnp.concatenate([hi, lo, hi], axis=1), carry[...])
        for k in range(span):
            at = pl.ds(pl.multiple_of((first + k) * chunk, chunk), chunk)
            convolved = full[:, k * LANES:(k + 1) * LANES].astype(BF16)
            gated[at, lanes] = (q_ref[at, lanes].astype(F32) * convolved.astype(F32)).astype(BF16)

    def early_inside(b, _):
        inside_step(b, 0)
        return 0

    def early_carry(b, _):
        carry_step(b, jnp.int32(0))
        return 0

    rest = 3 * lane_blocks
    batch = max(1, lane_blocks // 2)

    def late_step(item, _):
        b = item % lane_blocks
        first = (1 + item // lane_blocks) * span
        inside_step(b, first)
        carry_step(b, first)
        return 0

    group = lax.broadcasted_iota(jnp.int32, (groups, state, LANES), 0) * SHARE
    lane = lax.broadcasted_iota(jnp.int32, (groups, state, LANES), 2)
    gmask_ref[...] = jnp.where((lane >= group) & (lane < group + SHARE), 1.0, 0.0).reshape(modes, LANES)
    group = lax.broadcasted_iota(jnp.int32, (groups, modes), 0) * state
    lane = lax.broadcasted_iota(jnp.int32, (groups, modes), 1)
    smask_ref[...] = jnp.where((lane >= group) & (lane < group + state), 1.0, 0.0)
    loads[4].wait()
    loads[5].wait()
    lax.fori_loop(0, lane_blocks, table_step, 0)
    loads[0].wait()
    loads[1].wait()
    loads[2].start()
    loads[3].start()
    lax.fori_loop(0, lane_blocks, state_step, 0)
    lax.fori_loop(1, ctx - me, lambda d, _: (to_peer(d).start(), 0)[1], 0)
    lax.fori_loop(0, lane_blocks, taps_step, 0)
    lax.fori_loop(0, lane_blocks, early_inside, 0)
    lax.fori_loop(0, me, lambda j, _: (from_peer(j).wait_recv(), 0)[1], 0)
    loads[2].wait()
    lax.fori_loop(0, lane_blocks, early_carry, 0)
    loads[3].wait()

    def tile_rows(tile):
        return pl.ds(pl.multiple_of(tile * rows, rows), rows)

    def share(tile, dest):
        cols = pl.ds(pl.multiple_of(dest * width, width), width)
        return dot(gated[tile_rows(tile), :], w_ref[:, cols])

    def some_rows(u):
        return pl.ds(pl.multiple_of(u * some, some), some)

    def rightward(src, i, tile, u):
        return pltpu.make_async_remote_copy(
            src_ref=src, dst_ref=right_buf.at[i, tile, some_rows(u)], send_sem=right_send.at[i, tile, u],
            recv_sem=right_recv.at[i, tile, u], device_id={"tp": place + 1}, device_id_type=MESH)

    def leftward(src, i, tile, u):
        return pltpu.make_async_remote_copy(
            src_ref=src, dst_ref=left_buf.at[i, tile, some_rows(u)], send_sem=left_send.at[i, tile, u],
            recv_sem=left_recv.at[i, tile, u], device_id={"tp": place - 1}, device_id_type=MESH)

    def each(body):
        lax.fori_loop(0, subs, lambda u, _: (body(u), 0)[1], 0)

    def received(copy, buf, i, tile):
        each(lambda u: copy(buf.at[i, tile, some_rows(u)], i, tile, u).wait_recv())

    flows = ((place, rightward, right_buf, lambda d: d), (far, leftward, left_buf, lambda d: tp - 1 - d))

    def sums_step(flow, i, tile, go):
        role, copy, buf, physical = flow
        came = i - (role >= 2).astype(jnp.int32)
        dest = tp - 1 - i + jnp.maximum(role - 1, 0)

        @pl.when(go)
        def _():
            part[...] = share(tile, physical(dest))

        @pl.when(go & (role > 0))
        def _():
            def add(u):
                at = some_rows(u)
                copy(buf.at[came, tile, at], came, tile, u).wait_recv()
                buf[came, tile, at] = (part[at, :] + buf[came, tile, at].astype(F32)).astype(BF16)
                copy(buf.at[came, tile, at], i, tile, u).start()

            each(add)

        @pl.when(go & (role == 0))
        def _():
            buf[came, tile] = part[...].astype(BF16)
            each(lambda u: copy(buf.at[came, tile, some_rows(u)], i, tile, u).start())

    steps = early * inner

    def early_step(t, _):
        m = t // inner
        i = t % inner
        for flow in flows:
            sums_step(flow, i, m, i >= flow[0] - 1)

        @pl.when(is_helper & (t < inner))
        def _():
            spread_block(t)

        @pl.when(is_helper & (t >= steps - inner))
        def _():
            relay_block(t - (steps - inner))

        lax.fori_loop(jnp.minimum(t * batch, rest), jnp.minimum(t * batch + batch, rest), late_step, 0)
        return 0

    lax.fori_loop(0, steps, early_step, 0)
    lax.fori_loop(min(steps * batch, rest), rest, late_step, 0)

    def end_step(flow, m, i, to_right):
        role, copy, buf, physical = flow
        tile = early + m

        @pl.when((role == 0) & (i == 0))
        def _():
            def send(u):
                at = pl.ds(pl.multiple_of(tile * rows + u * some, some), some)
                copy(gated.at[at], 0, tile, u).start()

            each(send)

        @pl.when((role == 0) & (i == 1) & (m == 0))
        def _():
            hop(tp - 2, to_right).start()

        @pl.when((role == 0) & (i == 1) & (m > 0) & (m <= early))
        def _():
            buf[1, tile] = share(m - 1, physical(1)).astype(BF16)
            each(lambda u: copy(buf.at[1, tile, some_rows(u)], 1, tile, u).start())

    def helper_step(flow, m, i):
        role, copy, buf, physical = flow
        tile = early + m

        @pl.when(role == 1)
        def _():
            part[...] = share(tile, physical(tp - 1 - i))

            @pl.when(i == 0)
            def _():
                received(copy, buf, 0, tile)

            @pl.when(m == 0)
            def _():
                await_block(i)

            stage[i, m] = (part[...] + dot(buf[0, tile], extra[column_block(i, place == 1)])).astype(BF16)
            each(lambda u: copy(stage.at[i, m, some_rows(u)], i, tile, u).start())

    def late_sums(t, _):
        m = t // inner
        i = t % inner
        for flow, to_right in zip(flows, (True, False)):
            end_step(flow, m, i, to_right)
            helper_step(flow, m, i)
            sums_step(flow, i, early + m, (flow[0] >= 2) & (i >= flow[0] - 1))

        @pl.when(is_helper & (i == inner - 1) & (m == 1))
        def _():
            spread_block(tp - 2)

        @pl.when(is_helper & (i == inner - 1) & (m == late - 2))
        def _():
            relay_block(tp - 2)
        return 0

    lax.fori_loop(0, late * inner, late_sums, 0)

    def early_result(m, _):
        part[...] = share(m, place)
        for role, copy, buf, _physical in flows:
            @pl.when(role == 1)
            def _():
                received(copy, buf, 1, early + 1 + m)
                part[...] += buf[1, early + 1 + m].astype(F32)

            @pl.when(role >= 2)
            def _():
                received(copy, buf, inner - 1, m)
                part[...] += buf[inner - 1, m].astype(F32)

        out_ref[tile_rows(m), :] = part[...].astype(BF16)
        return 0

    lax.fori_loop(0, early, early_result, 0)

    @pl.when(is_helper)
    def _():
        await_block(tp - 2)

    def late_result(m, _):
        tile = early + m
        part[...] = share(tile, place)
        for role, copy, buf, _physical in flows:
            @pl.when(role == 1)
            def _():
                part[...] += dot(buf[0, tile], extra[column_block(tp - 2, place == 1)])

        for role, copy, buf, _physical in flows:
            @pl.when(role >= 2)
            def _():
                received(copy, buf, inner - 1, tile)
                part[...] += buf[inner - 1, tile].astype(F32)

        out_ref[tile_rows(tile), :] = part[...].astype(BF16)
        return 0

    lax.fori_loop(0, late, late_result, 0)

    def sent_step(t, _):
        tile = t // inner
        i = t % inner
        m = tile - early
        for role, copy, buf, _physical in flows:
            from_end = (m < 0) | (i == 0) | ((i == 1) & (m > 0) & (m <= early))

            @pl.when(((role == 0) & from_end) | ((role > 0) & (i >= role - 1)))
            def _():
                each(lambda u: copy(buf.at[i, tile, some_rows(u)], i, tile, u).wait_send())
        return 0

    lax.fori_loop(0, (early + late) * inner, sent_step, 0)
    lax.fori_loop(1, ctx - me, lambda d, _: (to_peer(d).wait_send(), 0)[1], 0)

    @pl.when((place == 0) | (far == 0))
    def _():
        lax.fori_loop(0, tp - 1, lambda o, _: (hop(o, place == 0).wait_send(), 0)[1], 0)

    @pl.when(is_helper)
    def _():
        for order in range(tp - 1):
            lax.fori_loop(1, chips, lambda d, _: (across(order, d).wait_send(), 0)[1], 0)
            lax.fori_loop(0, chips, lambda d, _: (beside(order, d).wait_send(), 0)[1], 0)


def on_device(ctx, tp, query, keys, values, residues, rates, w_out):
    block, width = keys.shape
    state = rates.shape[1]
    chunk = math.gcd(block, LANES)
    chunks = block // chunk
    span = chunks // 4
    groups = LANES // SHARE
    modes = groups * state
    lane_blocks = width // LANES
    early, late = 3, 5
    inner = tp - 2
    rows = block // (early + late)
    vmem = pl.BlockSpec(memory_space=pltpu.VMEM)
    hbm = pl.BlockSpec(memory_space=pltpu.HBM)
    dma = pltpu.SemaphoreType.DMA
    return pl.pallas_call(
        functools.partial(layer_kernel, ctx, tp, early, late, state, chunk),
        out_shape=jax.ShapeDtypeStruct((block, width), BF16),
        in_specs=[hbm] * 6,
        out_specs=vmem,
        scratch_shapes=[
            pltpu.VMEM((state, rates.shape[0]), F32),
            pltpu.VMEM((state, rates.shape[0]), F32),
            pltpu.VMEM((modes, LANES), F32),
            pltpu.VMEM((groups, modes), F32),
            pltpu.VMEM((block, width), BF16),
            pltpu.VMEM((block, width), BF16),
            pltpu.VMEM((block, width), BF16),
            pltpu.VMEM(w_out.shape, BF16),
            pltpu.VMEM((lane_blocks, modes, LANES), F32),
            pltpu.VMEM((lane_blocks, 8, modes), F32),
            pltpu.VMEM((lane_blocks, 8, modes), F32),
            pltpu.VMEM((block, width), BF16),
            pltpu.VMEM((ctx, state, width), F32),
            pltpu.VMEM((state, width), F32),
            pltpu.VMEM((chunks, state, width), F32),
            pltpu.VMEM((lane_blocks, chunk, span * LANES), F32),
            pltpu.VMEM((groups * chunk, span * LANES), BF16),
            pltpu.VMEM((lane_blocks, chunk, groups * chunk), BF16),
            pltpu.VMEM((3 * modes, span * LANES), BF16),
            pltpu.VMEM((tp - 1, width, width), BF16),
            pltpu.VMEM((inner, early + late, rows, width), BF16),
            pltpu.VMEM((inner, early + late, rows, width), BF16),
            pltpu.VMEM((inner, late, rows, width), BF16),
            pltpu.VMEM((rows, width), F32),
            dma((6,)),
            dma((ctx,)),
            dma((ctx,)),
            dma((tp - 1,)),
            dma((tp - 1,)),
            dma((tp - 1, ctx)),
            dma((tp - 1, ctx)),
            dma((inner, early + late, SUBS)),
            dma((inner, early + late, SUBS)),
            dma((inner, early + late, SUBS)),
            dma((inner, early + late, SUBS)),
        ],
        compiler_params=pltpu.CompilerParams(
            collective_id=0, has_side_effects=True, vmem_limit_bytes=50 * 2**20),
        cost_estimate=pl.CostEstimate(
            flops=4 * block * width * width * tp, bytes_accessed=24 * block * width, transcendentals=0),
        name="hyena_layer",
    )(query, keys, values, w_out, rates.T, residues.T)


def solution(mesh):
    in_specs = (P("ctx", "tp"), P("ctx", "tp"), P("ctx", "tp"), P(), P(), P("tp", None))
    return jax.shard_map(
        functools.partial(on_device, mesh.shape["ctx"], mesh.shape["tp"]),
        mesh=mesh, in_specs=in_specs, out_specs=P("ctx", "tp"), check_vma=False)
```

```python
import functools
import math

import jax
import jax.numpy as jnp
from jax import lax
from jax.experimental import pallas as pl
from jax.experimental.pallas import tpu as pltpu
from jax.sharding import PartitionSpec as P

SHARE = 16
LANES = 128
SUBS = 8
MESH = pl.DeviceIdType.MESH
F32 = jnp.float32
BF16 = jnp.bfloat16


def split(x):
    upper = x.astype(BF16)
    return upper, (x - upper.astype(F32)).astype(BF16)


def dot(a, b):
    return jnp.dot(a, b, preferred_element_type=F32)


def layer_kernel(ctx, tp, tiles, state, chunk, q_hbm, k_hbm, v_hbm, w_hbm, rates_hbm, residues_hbm,
                 out_ref, rates_ref, residues_ref, gmask_ref, smask_ref, q_ref, k_ref, v_ref, w_ref, columns, rate_rows, gain_rows, gated, states, own, before,
                 inside, wide, taps, carry, extra, right_buf, left_buf, stage, part, early_part, load_sem, state_send, state_recv, hop_send,
                 hop_recv, spread_send, spread_recv, right_send, right_recv, left_send, left_recv):
    block, width = out_ref.shape
    chunks = block // chunk
    span = chunks // 4
    lane_blocks = width // LANES
    groups = LANES // SHARE
    modes = groups * state
    rows = block // (2 * tiles)
    subs = SUBS
    some = rows // subs
    piece = width // ctx
    inner = tp - 2
    me = lax.axis_index("ctx")
    place = lax.axis_index("tp")
    far = tp - 1 - place
    has_left = place > 0
    has_right = far > 0
    is_helper = (place == 1) | (far == 1)

    loads = [pltpu.make_async_copy(src, dst, load_sem.at[i]) for i, (src, dst) in enumerate(
        [(k_hbm, k_ref), (v_hbm, v_ref), (q_hbm, q_ref), (w_hbm, w_ref), (rates_hbm, rates_ref),
         (residues_hbm, residues_ref)])]
    for at in (4, 5, 0, 1):
        loads[at].start()

    barrier = pltpu.get_barrier_semaphore()

    def greet(d, _):
        pl.semaphore_signal(barrier, inc=1, device_id={"ctx": lax.rem(me + d, ctx)}, device_id_type=MESH)
        return 0

    lax.fori_loop(1, ctx, greet, 0)

    @pl.when(has_left)
    def _():
        pl.semaphore_signal(barrier, inc=1, device_id={"tp": place - 1}, device_id_type=MESH)

    @pl.when(has_right)
    def _():
        pl.semaphore_signal(barrier, inc=1, device_id={"tp": place + 1}, device_id_type=MESH)

    pl.semaphore_wait(barrier, ctx - 1 + has_left.astype(jnp.int32) + has_right.astype(jnp.int32))

    def column_block(order, from_left):
        return jnp.where(from_left, tp - 2 - order, order)

    def piece_rows(j):
        return pl.ds(pl.multiple_of(j * piece, piece), piece)

    def hop(order, to_right):
        e = column_block(order, to_right)
        cols = pl.ds(pl.multiple_of(jnp.where(to_right, e + 1, e) * width, width), width)
        return pltpu.make_async_remote_copy(
            src_ref=w_hbm.at[piece_rows(me), cols], dst_ref=extra.at[e, piece_rows(me)],
            send_sem=hop_send.at[e], recv_sem=hop_recv.at[e],
            device_id={"tp": jnp.where(to_right, place + 1, place - 1)}, device_id_type=MESH)

    def hop_step(order, _):
        hop(order, place == 0).start()
        return 0

    @pl.when((place == 0) | (far == 0))
    def _():
        lax.fori_loop(0, tp - 1, hop_step, 0)

    chips = ctx // 2
    sibling = me + 1 - 2 * lax.rem(me, 2)

    def chip_peer(d):
        return lax.rem(me + 2 * d, ctx)

    def carried(order, j, send, peer):
        e = column_block(order, place == 1)
        return pltpu.make_async_remote_copy(
            src_ref=extra.at[e, piece_rows(j)], dst_ref=extra.at[e, piece_rows(j)],
            send_sem=spread_send.at[e, send], recv_sem=spread_recv.at[e, j],
            device_id={"ctx": peer}, device_id_type=MESH)

    def across(order, d):
        return carried(order, me, d, chip_peer(d))

    def beside(order, d):
        return carried(order, chip_peer(d), chips + d, sibling)

    def spread_block(order):
        e = column_block(order, place == 1)
        pltpu.make_async_remote_copy(
            src_ref=w_hbm.at[piece_rows(me), pl.ds(0, width)], dst_ref=extra.at[e, piece_rows(me)],
            send_sem=hop_send.at[e], recv_sem=hop_recv.at[e],
            device_id={"tp": jnp.where(place == 1, place - 1, place + 1)}, device_id_type=MESH).wait_recv()
        lax.fori_loop(1, chips, lambda d, _: (across(order, d).start(), 0)[1], 0)
        beside(order, 0).start()

    def relay_block(order):
        def relay(d, _):
            carried(order, chip_peer(d), d, chip_peer(d)).wait_recv()
            beside(order, d).start()
            return 0

        lax.fori_loop(1, chips, relay, 0)

    def await_block(order):
        def arrived(d, _):
            j = lax.rem(sibling + 2 * d, ctx)
            carried(order, j, chips + d, sibling).wait_recv()
            return 0

        lax.fori_loop(0, chips, arrived, 0)

    def product(k, lanes):
        at = pl.ds(pl.multiple_of(k * chunk, chunk), chunk)
        return (k_ref[at, lanes].astype(F32) * v_ref[at, lanes].astype(F32)).astype(BF16)

    def lanes_of(b):
        return pl.ds(pl.multiple_of(b * LANES, LANES), LANES)

    def spread_rows(ref, b):
        every = ref.shape[1]
        tall = jnp.concatenate([ref[...]] * groups, axis=0)
        lane = lax.broadcasted_iota(jnp.int32, (groups, state, every), 2)
        group = lax.broadcasted_iota(jnp.int32, (groups, state, every), 0)
        first = (place * lane_blocks + b) * groups
        chosen = jnp.where(lane == group + first, tall.reshape(groups, state, every), 0.0)
        column = chosen.sum(axis=2, keepdims=True).reshape(modes, 1)
        return jnp.broadcast_to(column, (modes, LANES))

    def table_step(b, _):
        rate = spread_rows(rates_ref, b)
        columns[b] = rate
        rate_rows[b] = rate.T[0:8, :]
        gain_rows[b] = (spread_rows(residues_ref, b) * jnp.sqrt(2.0 * rate)).T[0:8, :]
        return 0

    def rate_row(b):
        return rate_rows[b, 0:1, :]

    def gain_row(b):
        return gain_rows[b, 0:1, :]

    def rate_columns(b):
        return columns[b]

    def rate_lanes(b):
        return (rate_columns(b) * gmask_ref[...]).reshape(groups, state, LANES).sum(0)

    def state_step(b, _):
        lanes = lanes_of(b)
        tau = lax.broadcasted_iota(jnp.int32, (modes, chunk), 1).astype(F32)
        fading = jnp.concatenate(split(jnp.exp(-rate_columns(b) * (chunk - 1.0 - tau))), axis=0)
        decay = jnp.exp(-rate_lanes(b) * float(chunk))
        gmask = gmask_ref[...]
        fresh = dot(fading, jnp.concatenate([product(k, lanes) for k in range(chunks)], axis=1))
        fresh = fresh[:modes] + fresh[modes:]
        total = jnp.zeros((state, LANES), F32)
        for k in range(chunks):
            before[k, :, lanes] = total
            new = fresh[:, k * LANES:(k + 1) * LANES] * gmask
            total = total * decay + new.reshape(groups, state, LANES).sum(0)
        own[:, lanes] = total
        return 0


    def to_peer(d):
        return pltpu.make_async_remote_copy(
            src_ref=own, dst_ref=states.at[me], send_sem=state_send.at[d], recv_sem=state_recv.at[me],
            device_id={"ctx": lax.rem(me + d, ctx)}, device_id_type=MESH)

    def from_peer(j):
        return pltpu.make_async_remote_copy(
            src_ref=own, dst_ref=states.at[j], send_sem=state_send.at[0], recv_sem=state_recv.at[j],
            device_id={"ctx": j}, device_id_type=MESH)

    def taps_step(b, _):
        row = lax.broadcasted_iota(jnp.int32, (chunk, modes), 0).astype(F32)
        col = lax.broadcasted_iota(jnp.int32, (modes, chunk), 1).astype(F32)
        middle = chunk / 2.0
        falling = gain_row(b) * jnp.exp(-rate_row(b) * (row - middle))
        b_hi, b_lo = split(jnp.exp(rate_columns(b) * (col - middle)))
        causal = lax.broadcasted_iota(jnp.int32, (chunk, chunk), 0) >= lax.broadcasted_iota(
            jnp.int32, (chunk, chunk), 1)
        a_hi, a_lo = split(jnp.concatenate([falling * smask_ref[g:g + 1, :] for g in range(groups)], axis=0))
        tap = dot(jnp.concatenate([a_hi, a_lo, a_hi], axis=1), jnp.concatenate([b_hi, b_hi, b_lo], axis=0))
        for g in range(groups):
            own_tap = jnp.where(causal, tap[g * chunk:(g + 1) * chunk], 0.0)
            taps[b, :, g * chunk:(g + 1) * chunk] = own_tap.astype(BF16)
        return 0

    def inside_step(b, first):
        lanes = lanes_of(b)
        xs = [product(first + k, lanes) for k in range(span)]
        for g in range(groups):
            only = gmask_ref[g * state:g * state + 1, :].astype(BF16)
            for k in range(span):
                wide[g * chunk:(g + 1) * chunk, k * LANES:(k + 1) * LANES] = xs[k] * only
        inside[b] = dot(taps[b], wide[...])

    def carry_step(b, first):
        lanes = lanes_of(b)
        rlane = rate_lanes(b)
        along = jnp.exp(-rlane * float(block))
        decay = jnp.exp(-rlane * float(chunk))
        reached = lax.fori_loop(
            0, me, lambda j, r: r * along + states[j, :, lanes], jnp.zeros((state, LANES), F32))
        reached = reached * jnp.exp(-rlane * (chunk * first).astype(F32))
        gmask = gmask_ref[...]
        for k in range(span):
            entering = before[first + k, :, lanes] + reached
            reached = reached * decay
            hi, lo = split(jnp.concatenate([entering] * groups, axis=0) * gmask)
            at = slice(k * LANES, (k + 1) * LANES)
            carry[0:modes, at] = hi
            carry[modes:2 * modes, at] = hi
            carry[2 * modes:3 * modes, at] = lo
        row = lax.broadcasted_iota(jnp.int32, (chunk, modes), 0).astype(F32)
        hi, lo = split(gain_row(b) * jnp.exp(-rate_row(b) * (row + 1.0)))
        full = inside[b] + dot(jnp.concatenate([hi, lo, hi], axis=1), carry[...])
        for k in range(span):
            at = pl.ds(pl.multiple_of((first + k) * chunk, chunk), chunk)
            convolved = full[:, k * LANES:(k + 1) * LANES].astype(BF16)
            gated[at, lanes] = (q_ref[at, lanes].astype(F32) * convolved.astype(F32)).astype(BF16)

    def early_inside(b, _):
        inside_step(b, 0)
        return 0

    def early_carry(b, _):
        carry_step(b, jnp.int32(0))
        return 0

    rest = 3 * lane_blocks
    batch = lane_blocks

    def late_step(item, _):
        b = item % lane_blocks
        first = (1 + item // lane_blocks) * span
        inside_step(b, first)
        carry_step(b, first)
        return 0

    group = lax.broadcasted_iota(jnp.int32, (groups, state, LANES), 0) * SHARE
    lane = lax.broadcasted_iota(jnp.int32, (groups, state, LANES), 2)
    gmask_ref[...] = jnp.where((lane >= group) & (lane < group + SHARE), 1.0, 0.0).reshape(modes, LANES)
    group = lax.broadcasted_iota(jnp.int32, (groups, modes), 0) * state
    lane = lax.broadcasted_iota(jnp.int32, (groups, modes), 1)
    smask_ref[...] = jnp.where((lane >= group) & (lane < group + state), 1.0, 0.0)
    loads[4].wait()
    loads[5].wait()
    lax.fori_loop(0, lane_blocks, table_step, 0)
    loads[0].wait()
    loads[1].wait()
    loads[2].start()
    loads[3].start()
    lax.fori_loop(0, lane_blocks, state_step, 0)
    lax.fori_loop(1, ctx - me, lambda d, _: (to_peer(d).start(), 0)[1], 0)
    lax.fori_loop(0, lane_blocks, taps_step, 0)
    lax.fori_loop(0, lane_blocks, early_inside, 0)
    lax.fori_loop(0, me, lambda j, _: (from_peer(j).wait_recv(), 0)[1], 0)
    loads[2].wait()
    lax.fori_loop(0, lane_blocks, early_carry, 0)
    loads[3].wait()

    def early_tile(m):
        return pl.ds(pl.multiple_of(m * rows, rows), rows)

    def late_tile(m):
        return pl.ds(pl.multiple_of((tiles + m) * rows, rows), rows)

    def share(tile, dest):
        cols = pl.ds(pl.multiple_of(dest * width, width), width)
        return dot(gated[tile, :], w_ref[:, cols])

    def some_rows(u):
        return pl.ds(pl.multiple_of(u * some, some), some)

    def rightward(src, h, i, m, u):
        return pltpu.make_async_remote_copy(
            src_ref=src, dst_ref=right_buf.at[h, i, m, some_rows(u)], send_sem=right_send.at[h, i, m, u],
            recv_sem=right_recv.at[h, i, m, u], device_id={"tp": place + 1}, device_id_type=MESH)

    def leftward(src, h, i, m, u):
        return pltpu.make_async_remote_copy(
            src_ref=src, dst_ref=left_buf.at[h, i, m, some_rows(u)], send_sem=left_send.at[h, i, m, u],
            recv_sem=left_recv.at[h, i, m, u], device_id={"tp": place - 1}, device_id_type=MESH)

    def each(body):
        lax.fori_loop(0, subs, lambda u, _: (body(u), 0)[1], 0)

    def received(copy, buf, h, i, m, u):
        copy(buf.at[h, i, m, some_rows(u)], h, i, m, u).wait_recv()

    flows = ((place, rightward, right_buf, lambda d: d), (far, leftward, left_buf, lambda d: tp - 1 - d))

    def sums_step(flow, h, i, m, tile, go):
        role, copy, buf, physical = flow
        came = i - (role >= 2).astype(jnp.int32)
        dest = tp - 1 - i + jnp.maximum(role - 1, 0)

        @pl.when(go)
        def _():
            part[...] = share(tile, physical(dest))

        @pl.when(go & (role > 0))
        def _():
            def add(u):
                at = some_rows(u)
                received(copy, buf, h, came, m, u)
                buf[h, came, m, at] = (part[at, :] + buf[h, came, m, at].astype(F32)).astype(BF16)
                copy(buf.at[h, came, m, at], h, i, m, u).start()

            each(add)

        @pl.when(go & (role == 0))
        def _():
            buf[h, came, m] = part[...].astype(BF16)
            each(lambda u: copy(buf.at[h, came, m, some_rows(u)], h, i, m, u).start())

    steps = inner * tiles

    def early_step(t, _):
        i = t // tiles
        m = t % tiles
        for flow in flows:
            sums_step(flow, 0, i, m, early_tile(m), i >= flow[0] - 1)

        @pl.when(is_helper & (t < tp - 1))
        def _():
            spread_block(t)

        @pl.when(is_helper & (t >= steps - (tp - 1)))
        def _():
            relay_block(t - (steps - (tp - 1)))

        lax.fori_loop(jnp.minimum(t * batch, rest), jnp.minimum(t * batch + batch, rest), late_step, 0)
        return 0

    lax.fori_loop(0, steps, early_step, 0)
    lax.fori_loop(min(steps * batch, rest), rest, late_step, 0)

    def end_step(flow, i, m):
        role, copy, buf, physical = flow

        @pl.when((role == 0) & (i == 0))
        def _():
            def send(u):
                at = pl.ds(pl.multiple_of((tiles + m) * rows + u * some, some), some)
                copy(gated.at[at], 1, 0, m, u).start()

            each(send)

        @pl.when((role == 0) & (i == 1))
        def _():
            buf[1, 1, m] = share(early_tile(m), physical(1)).astype(BF16)
            each(lambda u: copy(buf.at[1, 1, m, some_rows(u)], 1, 1, m, u).start())

    def helper_step(flow, i, m):
        role, copy, buf, physical = flow

        @pl.when(role == 1)
        def _():
            part[...] = share(late_tile(m), physical(tp - 1 - i))

            @pl.when(i == 0)
            def _():
                each(lambda u: received(copy, buf, 1, 0, m, u))

            @pl.when(m == 0)
            def _():
                await_block(i)

            stage[i, m] = (part[...] + dot(buf[1, 0, m], extra[column_block(i, place == 1)])).astype(BF16)
            each(lambda u: copy(stage.at[i, m, some_rows(u)], 1, i, m, u).start())

    def late_sums(t, _):
        i = t // tiles
        m = t % tiles
        for flow in flows:
            end_step(flow, i, m)
            helper_step(flow, i, m)
            sums_step(flow, 1, i, m, late_tile(m), (flow[0] >= 2) & (i >= flow[0] - 1))
        return 0

    lax.fori_loop(0, steps, late_sums, 0)

    @pl.when(is_helper)
    def _():
        await_block(tp - 2)

    def last_step(m, _):
        part[...] = share(late_tile(m), place)
        early_part[...] = share(early_tile(m), place)
        for role, copy, buf, _physical in flows:
            @pl.when(role == 1)
            def _():
                part[...] += dot(buf[1, 0, m], extra[column_block(tp - 2, place == 1)])

        for role, copy, buf, _physical in flows:
            @pl.when(role == 1)
            def _():
                each(lambda u: received(copy, buf, 1, 1, m, u))
                early_part[...] += buf[1, 1, m].astype(F32)

            @pl.when(role >= 2)
            def _():
                each(lambda u: received(copy, buf, 0, inner - 1, m, u))
                early_part[...] += buf[0, inner - 1, m].astype(F32)
                each(lambda u: received(copy, buf, 1, inner - 1, m, u))
                part[...] += buf[1, inner - 1, m].astype(F32)

        out_ref[late_tile(m), :] = part[...].astype(BF16)
        out_ref[early_tile(m), :] = early_part[...].astype(BF16)
        return 0

    lax.fori_loop(0, tiles, last_step, 0)

    def sent_step(t, _):
        i = t // tiles
        m = t % tiles
        for role, copy, buf, _physical in flows:
            for h in range(2):
                early_end = (role == 0) if h == 0 else (role == 0) & (i < 2)

                @pl.when(early_end | ((role > 0) & (i >= role - 1)))
                def _():
                    each(lambda u: copy(buf.at[h, i, m, some_rows(u)], h, i, m, u).wait_send())
        return 0

    lax.fori_loop(0, steps, sent_step, 0)
    lax.fori_loop(1, ctx - me, lambda d, _: (to_peer(d).wait_send(), 0)[1], 0)

    @pl.when((place == 0) | (far == 0))
    def _():
        lax.fori_loop(0, tp - 1, lambda o, _: (hop(o, place == 0).wait_send(), 0)[1], 0)

    @pl.when(is_helper)
    def _():
        for order in range(tp - 1):
            lax.fori_loop(1, chips, lambda d, _: (across(order, d).wait_send(), 0)[1], 0)
            lax.fori_loop(0, chips, lambda d, _: (beside(order, d).wait_send(), 0)[1], 0)


def on_device(ctx, tp, query, keys, values, residues, rates, w_out):
    block, width = keys.shape
    state = rates.shape[1]
    chunk = math.gcd(block, LANES)
    chunks = block // chunk
    span = chunks // 4
    groups = LANES // SHARE
    modes = groups * state
    lane_blocks = width // LANES
    tiles = 2
    inner = tp - 2
    rows = block // (2 * tiles)
    vmem = pl.BlockSpec(memory_space=pltpu.VMEM)
    hbm = pl.BlockSpec(memory_space=pltpu.HBM)
    dma = pltpu.SemaphoreType.DMA
    return pl.pallas_call(
        functools.partial(layer_kernel, ctx, tp, tiles, state, chunk),
        out_shape=jax.ShapeDtypeStruct((block, width), BF16),
        in_specs=[hbm] * 6,
        out_specs=vmem,
        scratch_shapes=[
            pltpu.VMEM((state, rates.shape[0]), F32),
            pltpu.VMEM((state, rates.shape[0]), F32),
            pltpu.VMEM((modes, LANES), F32),
            pltpu.VMEM((groups, modes), F32),
            pltpu.VMEM((block, width), BF16),
            pltpu.VMEM((block, width), BF16),
            pltpu.VMEM((block, width), BF16),
            pltpu.VMEM(w_out.shape, BF16),
            pltpu.VMEM((lane_blocks, modes, LANES), F32),
            pltpu.VMEM((lane_blocks, 8, modes), F32),
            pltpu.VMEM((lane_blocks, 8, modes), F32),
            pltpu.VMEM((block, width), BF16),
            pltpu.VMEM((ctx, state, width), F32),
            pltpu.VMEM((state, width), F32),
            pltpu.VMEM((chunks, state, width), F32),
            pltpu.VMEM((lane_blocks, chunk, span * LANES), F32),
            pltpu.VMEM((groups * chunk, span * LANES), BF16),
            pltpu.VMEM((lane_blocks, chunk, groups * chunk), BF16),
            pltpu.VMEM((3 * modes, span * LANES), BF16),
            pltpu.VMEM((tp - 1, width, width), BF16),
            pltpu.VMEM((2, inner, tiles, rows, width), BF16),
            pltpu.VMEM((2, inner, tiles, rows, width), BF16),
            pltpu.VMEM((inner, tiles, rows, width), BF16),
            pltpu.VMEM((rows, width), F32),
            pltpu.VMEM((rows, width), F32),
            dma((6,)),
            dma((ctx,)),
            dma((ctx,)),
            dma((tp - 1,)),
            dma((tp - 1,)),
            dma((tp - 1, ctx)),
            dma((tp - 1, ctx)),
            dma((2, inner, tiles, SUBS)),
            dma((2, inner, tiles, SUBS)),
            dma((2, inner, tiles, SUBS)),
            dma((2, inner, tiles, SUBS)),
        ],
        compiler_params=pltpu.CompilerParams(
            collective_id=0, has_side_effects=True, vmem_limit_bytes=50 * 2**20),
        cost_estimate=pl.CostEstimate(
            flops=4 * block * width * width * tp, bytes_accessed=24 * block * width, transcendentals=0),
        name="hyena_layer",
    )(query, keys, values, w_out, rates.T, residues.T)


def solution(mesh):
    in_specs = (P("ctx", "tp"), P("ctx", "tp"), P("ctx", "tp"), P(), P(), P("tp", None))
    return jax.shard_map(
        functools.partial(on_device, mesh.shape["ctx"], mesh.shape["tp"]),
        mesh=mesh, in_specs=in_specs, out_specs=P("ctx", "tp"), check_vma=False)
```

```python
import functools
import math

import jax
import jax.numpy as jnp
from jax import lax
from jax.experimental import pallas as pl
from jax.experimental.pallas import tpu as pltpu
from jax.sharding import PartitionSpec as P

SHARE = 16
LANES = 128
SUBS = 2
MESH = pl.DeviceIdType.MESH
F32 = jnp.float32
BF16 = jnp.bfloat16


def split(x):
    upper = x.astype(BF16)
    return upper, (x - upper.astype(F32)).astype(BF16)


def dot(a, b):
    return jnp.dot(a, b, preferred_element_type=F32)


def layer_kernel(ctx, tp, tiles, state, chunk, q_hbm, k_hbm, v_hbm, w_hbm, rates_hbm, residues_hbm,
                 out_ref, rates_ref, residues_ref, gmask_ref, smask_ref, q_ref, k_ref, v_ref, w_ref, columns, rate_rows, gain_rows, gated, states, own, before,
                 inside, wide, taps, carry, extra, right_buf, left_buf, stage, part, early_part, load_sem, state_send, state_recv, hop_send,
                 hop_recv, spread_send, spread_recv, right_send, right_recv, left_send, left_recv):
    block, width = out_ref.shape
    chunks = block // chunk
    span = chunks // 4
    lane_blocks = width // LANES
    groups = LANES // SHARE
    modes = groups * state
    rows = block // (2 * tiles)
    subs = SUBS
    some = rows // subs
    piece = width // ctx
    inner = tp - 2
    me = lax.axis_index("ctx")
    place = lax.axis_index("tp")
    far = tp - 1 - place
    has_left = place > 0
    has_right = far > 0
    is_helper = (place == 1) | (far == 1)

    loads = [pltpu.make_async_copy(src, dst, load_sem.at[i]) for i, (src, dst) in enumerate(
        [(k_hbm, k_ref), (v_hbm, v_ref), (q_hbm, q_ref), (w_hbm, w_ref), (rates_hbm, rates_ref),
         (residues_hbm, residues_ref)])]
    for at in (4, 5, 0, 1):
        loads[at].start()

    barrier = pltpu.get_barrier_semaphore()

    def greet(d, _):
        pl.semaphore_signal(barrier, inc=1, device_id={"ctx": lax.rem(me + d, ctx)}, device_id_type=MESH)
        return 0

    lax.fori_loop(1, ctx, greet, 0)

    @pl.when(has_left)
    def _():
        pl.semaphore_signal(barrier, inc=1, device_id={"tp": place - 1}, device_id_type=MESH)

    @pl.when(has_right)
    def _():
        pl.semaphore_signal(barrier, inc=1, device_id={"tp": place + 1}, device_id_type=MESH)

    pl.semaphore_wait(barrier, ctx - 1 + has_left.astype(jnp.int32) + has_right.astype(jnp.int32))

    def column_block(order, from_left):
        return jnp.where(from_left, tp - 2 - order, order)

    def piece_rows(j):
        return pl.ds(pl.multiple_of(j * piece, piece), piece)

    def hop(order, to_right):
        e = column_block(order, to_right)
        cols = pl.ds(pl.multiple_of(jnp.where(to_right, e + 1, e) * width, width), width)
        return pltpu.make_async_remote_copy(
            src_ref=w_hbm.at[piece_rows(me), cols], dst_ref=extra.at[e, piece_rows(me)],
            send_sem=hop_send.at[e], recv_sem=hop_recv.at[e],
            device_id={"tp": jnp.where(to_right, place + 1, place - 1)}, device_id_type=MESH)

    def hop_step(order, _):
        hop(order, place == 0).start()
        return 0

    @pl.when((place == 0) | (far == 0))
    def _():
        lax.fori_loop(0, tp - 1, hop_step, 0)

    chips = ctx // 2
    sibling = me + 1 - 2 * lax.rem(me, 2)

    def chip_peer(d):
        return lax.rem(me + 2 * d, ctx)

    def carried(order, j, send, peer):
        e = column_block(order, place == 1)
        return pltpu.make_async_remote_copy(
            src_ref=extra.at[e, piece_rows(j)], dst_ref=extra.at[e, piece_rows(j)],
            send_sem=spread_send.at[e, send], recv_sem=spread_recv.at[e, j],
            device_id={"ctx": peer}, device_id_type=MESH)

    def across(order, d):
        return carried(order, me, d, chip_peer(d))

    def beside(order, d):
        return carried(order, chip_peer(d), chips + d, sibling)

    def spread_block(order):
        e = column_block(order, place == 1)
        pltpu.make_async_remote_copy(
            src_ref=w_hbm.at[piece_rows(me), pl.ds(0, width)], dst_ref=extra.at[e, piece_rows(me)],
            send_sem=hop_send.at[e], recv_sem=hop_recv.at[e],
            device_id={"tp": jnp.where(place == 1, place - 1, place + 1)}, device_id_type=MESH).wait_recv()
        lax.fori_loop(1, chips, lambda d, _: (across(order, d).start(), 0)[1], 0)
        beside(order, 0).start()

    def relay_block(order):
        def relay(d, _):
            carried(order, chip_peer(d), d, chip_peer(d)).wait_recv()
            beside(order, d).start()
            return 0

        lax.fori_loop(1, chips, relay, 0)

    def await_block(order):
        def arrived(d, _):
            j = lax.rem(sibling + 2 * d, ctx)
            carried(order, j, chips + d, sibling).wait_recv()
            return 0

        lax.fori_loop(0, chips, arrived, 0)

    def product(k, lanes):
        at = pl.ds(pl.multiple_of(k * chunk, chunk), chunk)
        return (k_ref[at, lanes].astype(F32) * v_ref[at, lanes].astype(F32)).astype(BF16)

    def lanes_of(b):
        return pl.ds(pl.multiple_of(b * LANES, LANES), LANES)

    def spread_rows(ref, b):
        every = ref.shape[1]
        tall = jnp.concatenate([ref[...]] * groups, axis=0)
        lane = lax.broadcasted_iota(jnp.int32, (groups, state, every), 2)
        group = lax.broadcasted_iota(jnp.int32, (groups, state, every), 0)
        first = (place * lane_blocks + b) * groups
        chosen = jnp.where(lane == group + first, tall.reshape(groups, state, every), 0.0)
        column = chosen.sum(axis=2, keepdims=True).reshape(modes, 1)
        return jnp.broadcast_to(column, (modes, LANES))

    def table_step(b, _):
        rate = spread_rows(rates_ref, b)
        columns[b] = rate
        rate_rows[b] = rate.T[0:8, :]
        gain_rows[b] = (spread_rows(residues_ref, b) * jnp.sqrt(2.0 * rate)).T[0:8, :]
        return 0

    def rate_row(b):
        return rate_rows[b, 0:1, :]

    def gain_row(b):
        return gain_rows[b, 0:1, :]

    def rate_columns(b):
        return columns[b]

    def rate_lanes(b):
        return (rate_columns(b) * gmask_ref[...]).reshape(groups, state, LANES).sum(0)

    def state_step(b, _):
        lanes = lanes_of(b)
        tau = lax.broadcasted_iota(jnp.int32, (modes, chunk), 1).astype(F32)
        fading = jnp.concatenate(split(jnp.exp(-rate_columns(b) * (chunk - 1.0 - tau))), axis=0)
        decay = jnp.exp(-rate_lanes(b) * float(chunk))
        gmask = gmask_ref[...]
        fresh = dot(fading, jnp.concatenate([product(k, lanes) for k in range(chunks)], axis=1))
        fresh = fresh[:modes] + fresh[modes:]
        total = jnp.zeros((state, LANES), F32)
        for k in range(chunks):
            before[k, :, lanes] = total
            new = fresh[:, k * LANES:(k + 1) * LANES] * gmask
            total = total * decay + new.reshape(groups, state, LANES).sum(0)
        own[:, lanes] = total
        return 0


    def to_peer(d):
        return pltpu.make_async_remote_copy(
            src_ref=own, dst_ref=states.at[me], send_sem=state_send.at[d], recv_sem=state_recv.at[me],
            device_id={"ctx": lax.rem(me + d, ctx)}, device_id_type=MESH)

    def from_peer(j):
        return pltpu.make_async_remote_copy(
            src_ref=own, dst_ref=states.at[j], send_sem=state_send.at[0], recv_sem=state_recv.at[j],
            device_id={"ctx": j}, device_id_type=MESH)

    def taps_step(b, _):
        row = lax.broadcasted_iota(jnp.int32, (chunk, modes), 0).astype(F32)
        col = lax.broadcasted_iota(jnp.int32, (modes, chunk), 1).astype(F32)
        middle = chunk / 2.0
        falling = gain_row(b) * jnp.exp(-rate_row(b) * (row - middle))
        b_hi, b_lo = split(jnp.exp(rate_columns(b) * (col - middle)))
        causal = lax.broadcasted_iota(jnp.int32, (chunk, chunk), 0) >= lax.broadcasted_iota(
            jnp.int32, (chunk, chunk), 1)
        a_hi, a_lo = split(jnp.concatenate([falling * smask_ref[g:g + 1, :] for g in range(groups)], axis=0))
        tap = dot(jnp.concatenate([a_hi, a_lo, a_hi], axis=1), jnp.concatenate([b_hi, b_hi, b_lo], axis=0))
        for g in range(groups):
            own_tap = jnp.where(causal, tap[g * chunk:(g + 1) * chunk], 0.0)
            taps[b, :, g * chunk:(g + 1) * chunk] = own_tap.astype(BF16)
        return 0

    def inside_step(b, first):
        lanes = lanes_of(b)
        xs = [product(first + k, lanes) for k in range(span)]
        for g in range(groups):
            only = gmask_ref[g * state:g * state + 1, :].astype(BF16)
            for k in range(span):
                wide[g * chunk:(g + 1) * chunk, k * LANES:(k + 1) * LANES] = xs[k] * only
        inside[b] = dot(taps[b], wide[...])

    def carry_step(b, first):
        lanes = lanes_of(b)
        rlane = rate_lanes(b)
        along = jnp.exp(-rlane * float(block))
        decay = jnp.exp(-rlane * float(chunk))
        reached = lax.fori_loop(
            0, me, lambda j, r: r * along + states[j, :, lanes], jnp.zeros((state, LANES), F32))
        reached = reached * jnp.exp(-rlane * (chunk * first).astype(F32))
        gmask = gmask_ref[...]
        for k in range(span):
            entering = before[first + k, :, lanes] + reached
            reached = reached * decay
            hi, lo = split(jnp.concatenate([entering] * groups, axis=0) * gmask)
            at = slice(k * LANES, (k + 1) * LANES)
            carry[0:modes, at] = hi
            carry[modes:2 * modes, at] = hi
            carry[2 * modes:3 * modes, at] = lo
        row = lax.broadcasted_iota(jnp.int32, (chunk, modes), 0).astype(F32)
        hi, lo = split(gain_row(b) * jnp.exp(-rate_row(b) * (row + 1.0)))
        full = inside[b] + dot(jnp.concatenate([hi, lo, hi], axis=1), carry[...])
        for k in range(span):
            at = pl.ds(pl.multiple_of((first + k) * chunk, chunk), chunk)
            convolved = full[:, k * LANES:(k + 1) * LANES].astype(BF16)
            gated[at, lanes] = (q_ref[at, lanes].astype(F32) * convolved.astype(F32)).astype(BF16)

    def early_inside(b, _):
        inside_step(b, 0)
        return 0

    def early_carry(b, _):
        carry_step(b, jnp.int32(0))
        return 0

    rest = 3 * lane_blocks
    batch = max(1, lane_blocks // 2)

    def late_step(item, _):
        b = item % lane_blocks
        first = (1 + item // lane_blocks) * span
        inside_step(b, first)
        carry_step(b, first)
        return 0

    group = lax.broadcasted_iota(jnp.int32, (groups, state, LANES), 0) * SHARE
    lane = lax.broadcasted_iota(jnp.int32, (groups, state, LANES), 2)
    gmask_ref[...] = jnp.where((lane >= group) & (lane < group + SHARE), 1.0, 0.0).reshape(modes, LANES)
    group = lax.broadcasted_iota(jnp.int32, (groups, modes), 0) * state
    lane = lax.broadcasted_iota(jnp.int32, (groups, modes), 1)
    smask_ref[...] = jnp.where((lane >= group) & (lane < group + state), 1.0, 0.0)
    loads[4].wait()
    loads[5].wait()
    lax.fori_loop(0, lane_blocks, table_step, 0)
    loads[0].wait()
    loads[1].wait()
    loads[2].start()
    loads[3].start()
    lax.fori_loop(0, lane_blocks, state_step, 0)
    lax.fori_loop(1, ctx - me, lambda d, _: (to_peer(d).start(), 0)[1], 0)
    lax.fori_loop(0, lane_blocks, taps_step, 0)
    lax.fori_loop(0, lane_blocks, early_inside, 0)
    lax.fori_loop(0, me, lambda j, _: (from_peer(j).wait_recv(), 0)[1], 0)
    loads[2].wait()
    lax.fori_loop(0, lane_blocks, early_carry, 0)
    loads[3].wait()

    def early_tile(m):
        return pl.ds(pl.multiple_of(m * rows, rows), rows)

    def late_tile(m):
        return pl.ds(pl.multiple_of((tiles + m) * rows, rows), rows)

    def share(tile, dest):
        cols = pl.ds(pl.multiple_of(dest * width, width), width)
        return dot(gated[tile, :], w_ref[:, cols])

    def some_rows(u):
        return pl.ds(pl.multiple_of(u * some, some), some)

    def rightward(src, h, i, m, u):
        return pltpu.make_async_remote_copy(
            src_ref=src, dst_ref=right_buf.at[h, i, m, some_rows(u)], send_sem=right_send.at[h, i, m, u],
            recv_sem=right_recv.at[h, i, m, u], device_id={"tp": place + 1}, device_id_type=MESH)

    def leftward(src, h, i, m, u):
        return pltpu.make_async_remote_copy(
            src_ref=src, dst_ref=left_buf.at[h, i, m, some_rows(u)], send_sem=left_send.at[h, i, m, u],
            recv_sem=left_recv.at[h, i, m, u], device_id={"tp": place - 1}, device_id_type=MESH)

    def each(body):
        lax.fori_loop(0, subs, lambda u, _: (body(u), 0)[1], 0)

    def received(copy, buf, h, i, m, u):
        copy(buf.at[h, i, m, some_rows(u)], h, i, m, u).wait_recv()

    flows = ((place, rightward, right_buf, lambda d: d), (far, leftward, left_buf, lambda d: tp - 1 - d))

    def sums_step(flow, h, i, m, tile, go):
        role, copy, buf, physical = flow
        came = i - (role >= 2).astype(jnp.int32)
        dest = tp - 1 - i + jnp.maximum(role - 1, 0)

        @pl.when(go)
        def _():
            part[...] = share(tile, physical(dest))

        @pl.when(go & (role > 0))
        def _():
            def add(u):
                at = some_rows(u)
                received(copy, buf, h, came, m, u)
                buf[h, came, m, at] = (part[at, :] + buf[h, came, m, at].astype(F32)).astype(BF16)
                copy(buf.at[h, came, m, at], h, i, m, u).start()

            each(add)

        @pl.when(go & (role == 0))
        def _():
            buf[h, came, m] = part[...].astype(BF16)
            each(lambda u: copy(buf.at[h, came, m, some_rows(u)], h, i, m, u).start())

    steps = inner * tiles

    def early_step(t, _):
        i = t // tiles
        m = t % tiles
        for flow in flows:
            sums_step(flow, 0, i, m, early_tile(m), i >= flow[0] - 1)

        @pl.when(is_helper & (t < tp - 1))
        def _():
            spread_block(t)

        @pl.when(is_helper & (t >= steps - (tp - 1)))
        def _():
            relay_block(t - (steps - (tp - 1)))

        lax.fori_loop(jnp.minimum(t * batch, rest), jnp.minimum(t * batch + batch, rest), late_step, 0)
        return 0

    lax.fori_loop(0, steps, early_step, 0)
    lax.fori_loop(min(steps * batch, rest), rest, late_step, 0)

    def end_step(flow, i, m):
        role, copy, buf, physical = flow

        @pl.when((role == 0) & (i == 0))
        def _():
            def send(u):
                at = pl.ds(pl.multiple_of((tiles + m) * rows + u * some, some), some)
                copy(gated.at[at], 1, 0, m, u).start()

            each(send)

        @pl.when((role == 0) & (i == 1))
        def _():
            buf[1, 1, m] = share(early_tile(m), physical(1)).astype(BF16)
            each(lambda u: copy(buf.at[1, 1, m, some_rows(u)], 1, 1, m, u).start())

    def helper_step(flow, i, m):
        role, copy, buf, physical = flow

        @pl.when(role == 1)
        def _():
            part[...] = share(late_tile(m), physical(tp - 1 - i))

            @pl.when(i == 0)
            def _():
                each(lambda u: received(copy, buf, 1, 0, m, u))

            @pl.when(m == 0)
            def _():
                await_block(i)

            stage[i, m] = (part[...] + dot(buf[1, 0, m], extra[column_block(i, place == 1)])).astype(BF16)
            each(lambda u: copy(stage.at[i, m, some_rows(u)], 1, i, m, u).start())

    def late_sums(t, _):
        i = t // tiles
        m = t % tiles
        for flow in flows:
            end_step(flow, i, m)
            helper_step(flow, i, m)
            sums_step(flow, 1, i, m, late_tile(m), (flow[0] >= 2) & (i >= flow[0] - 1))
        return 0

    lax.fori_loop(0, steps, late_sums, 0)

    @pl.when(is_helper)
    def _():
        await_block(tp - 2)

    def last_step(m, _):
        part[...] = share(late_tile(m), place)
        early_part[...] = share(early_tile(m), place)
        for role, copy, buf, _physical in flows:
            @pl.when(role == 1)
            def _():
                part[...] += dot(buf[1, 0, m], extra[column_block(tp - 2, place == 1)])

        for role, copy, buf, _physical in flows:
            @pl.when(role == 1)
            def _():
                each(lambda u: received(copy, buf, 1, 1, m, u))
                early_part[...] += buf[1, 1, m].astype(F32)

            @pl.when(role >= 2)
            def _():
                each(lambda u: received(copy, buf, 0, inner - 1, m, u))
                early_part[...] += buf[0, inner - 1, m].astype(F32)
                each(lambda u: received(copy, buf, 1, inner - 1, m, u))
                part[...] += buf[1, inner - 1, m].astype(F32)

        out_ref[late_tile(m), :] = part[...].astype(BF16)
        out_ref[early_tile(m), :] = early_part[...].astype(BF16)
        return 0

    lax.fori_loop(0, tiles, last_step, 0)

    def sent_step(t, _):
        i = t // tiles
        m = t % tiles
        for role, copy, buf, _physical in flows:
            for h in range(2):
                early_end = (role == 0) if h == 0 else (role == 0) & (i < 2)

                @pl.when(early_end | ((role > 0) & (i >= role - 1)))
                def _():
                    each(lambda u: copy(buf.at[h, i, m, some_rows(u)], h, i, m, u).wait_send())
        return 0

    lax.fori_loop(0, steps, sent_step, 0)
    lax.fori_loop(1, ctx - me, lambda d, _: (to_peer(d).wait_send(), 0)[1], 0)

    @pl.when((place == 0) | (far == 0))
    def _():
        lax.fori_loop(0, tp - 1, lambda o, _: (hop(o, place == 0).wait_send(), 0)[1], 0)

    @pl.when(is_helper)
    def _():
        for order in range(tp - 1):
            lax.fori_loop(1, chips, lambda d, _: (across(order, d).wait_send(), 0)[1], 0)
            lax.fori_loop(0, chips, lambda d, _: (beside(order, d).wait_send(), 0)[1], 0)


def on_device(ctx, tp, query, keys, values, residues, rates, w_out):
    block, width = keys.shape
    state = rates.shape[1]
    chunk = math.gcd(block, LANES)
    chunks = block // chunk
    span = chunks // 4
    groups = LANES // SHARE
    modes = groups * state
    lane_blocks = width // LANES
    tiles = 8
    inner = tp - 2
    rows = block // (2 * tiles)
    vmem = pl.BlockSpec(memory_space=pltpu.VMEM)
    hbm = pl.BlockSpec(memory_space=pltpu.HBM)
    dma = pltpu.SemaphoreType.DMA
    return pl.pallas_call(
        functools.partial(layer_kernel, ctx, tp, tiles, state, chunk),
        out_shape=jax.ShapeDtypeStruct((block, width), BF16),
        in_specs=[hbm] * 6,
        out_specs=vmem,
        scratch_shapes=[
            pltpu.VMEM((state, rates.shape[0]), F32),
            pltpu.VMEM((state, rates.shape[0]), F32),
            pltpu.VMEM((modes, LANES), F32),
            pltpu.VMEM((groups, modes), F32),
            pltpu.VMEM((block, width), BF16),
            pltpu.VMEM((block, width), BF16),
            pltpu.VMEM((block, width), BF16),
            pltpu.VMEM(w_out.shape, BF16),
            pltpu.VMEM((lane_blocks, modes, LANES), F32),
            pltpu.VMEM((lane_blocks, 8, modes), F32),
            pltpu.VMEM((lane_blocks, 8, modes), F32),
            pltpu.VMEM((block, width), BF16),
            pltpu.VMEM((ctx, state, width), F32),
            pltpu.VMEM((state, width), F32),
            pltpu.VMEM((chunks, state, width), F32),
            pltpu.VMEM((lane_blocks, chunk, span * LANES), F32),
            pltpu.VMEM((groups * chunk, span * LANES), BF16),
            pltpu.VMEM((lane_blocks, chunk, groups * chunk), BF16),
            pltpu.VMEM((3 * modes, span * LANES), BF16),
            pltpu.VMEM((tp - 1, width, width), BF16),
            pltpu.VMEM((2, inner, tiles, rows, width), BF16),
            pltpu.VMEM((2, inner, tiles, rows, width), BF16),
            pltpu.VMEM((inner, tiles, rows, width), BF16),
            pltpu.VMEM((rows, width), F32),
            pltpu.VMEM((rows, width), F32),
            dma((6,)),
            dma((ctx,)),
            dma((ctx,)),
            dma((tp - 1,)),
            dma((tp - 1,)),
            dma((tp - 1, ctx)),
            dma((tp - 1, ctx)),
            dma((2, inner, tiles, SUBS)),
            dma((2, inner, tiles, SUBS)),
            dma((2, inner, tiles, SUBS)),
            dma((2, inner, tiles, SUBS)),
        ],
        compiler_params=pltpu.CompilerParams(
            collective_id=0, has_side_effects=True, vmem_limit_bytes=50 * 2**20),
        cost_estimate=pl.CostEstimate(
            flops=4 * block * width * width * tp, bytes_accessed=24 * block * width, transcendentals=0),
        name="hyena_layer",
    )(query, keys, values, w_out, rates.T, residues.T)


def solution(mesh):
    in_specs = (P("ctx", "tp"), P("ctx", "tp"), P("ctx", "tp"), P(), P(), P("tp", None))
    return jax.shard_map(
        functools.partial(on_device, mesh.shape["ctx"], mesh.shape["tp"]),
        mesh=mesh, in_specs=in_specs, out_specs=P("ctx", "tp"), check_vma=False)
```
